256 devices in a mesh: tgt: 32 (over z_lo, y, core), src: 8 (over x, z_hi).
Axes of the slice: x: 4, y: 4, z: 8 (z_hi: 2, z_lo: 4; z = z_hi * 4 + z_lo), core: 2. Of those that a mesh axis runs over, the one named last changes fastest.
Arguments:
- positions: float32 [1024, 3, 642], P(('tgt', 'src')), may hold values from -1.1 to 358.4, as said below
- weights: float32 [1024, 642], P(('tgt', 'src')), may hold values from 0.0062305294 to 0.062305298
- density: float32 [1024, 3, 642], P(('tgt', 'src')), may hold values from -6 to 6
- near_source: int32 [1024, 8], P(('tgt', 'src')), may hold values from -1 to 1023, as said below
- couplings: bfloat16 [1024, 1024, 16, 16], P('tgt', 'src'), may hold values from -0.046875 to 0.046875
- source_basis: bfloat16 [1024, 16, 3, 642], P(('tgt', 'src')), may hold values from -0.125 to 0.125
- target_basis: bfloat16 [1024, 16, 3, 642], P(('tgt', 'src')), may hold values from -1.5 to 1.5
Outputs:
- velocity: float32 [1024, 3, 642], P(('tgt', 'src'))
The draws below stay inside these ranges and needn't reach their ends.
Inputs may be any that keep to these rules, and one draw needn't show every extreme that they name: `positions`: nodes of two different bodies are at least 0.1 apart. `near_source`: row i holds between 1 and 8 distinct bodies other than i, all in the same block of 32 consecutive bodies as i or in the block just before or after it; the used slots come first and the rest hold -1. Some rows use all 8 slots.
All inputs are finite; a program needn't handle non-finite values.
Results may differ from the reference program's by a relative error of at most 0.0033.
Values may be sent and summed in bfloat16 or wider, within the bound.
A program may use at most 64 MiB of HBM per device.

```python
import math
import jax
import jax.numpy as jnp
from jax import lax

P_SIZE = 642
RANK = 16
NEAR = 8
TGT_BODIES = 32
BODIES = 1024


def draw_positions(key, part):
    key = jax.random.fold_in(key, 11)
    keys = jax.random.split(key, 4)
    height = jax.random.uniform(keys[0], (BODIES, P_SIZE), jnp.float32, -1.0, 1.0)
    angle_turn = jax.random.uniform(keys[1], (BODIES, P_SIZE), jnp.float32, -math.pi, math.pi)
    radius = jax.random.uniform(keys[2], (BODIES, P_SIZE), jnp.float32, 0.75, 1.0)
    centre = jax.random.uniform(keys[3], (BODIES, 2), jnp.float32, -0.05, 0.05)
    index_all = jnp.arange(BODIES, dtype=jnp.int32)
    layer = (index_all // 2).astype(jnp.float32)[:, None]
    column_side = (index_all % 2).astype(jnp.float32)[:, None]
    circle = jnp.sqrt(jnp.maximum(1.0 - height * height, 0.0))
    along_x = 0.7 * layer + 0.3 * radius * height
    along_y = 2.2 * column_side + centre[:, 0:1] + radius * circle * jnp.cos(angle_turn)
    along_z = centre[:, 1:2] + radius * circle * jnp.sin(angle_turn)
    return jnp.stack([along_x, along_y, along_z], axis=1).astype(jnp.float32)


def draw_near_source(key, part):
    key = jax.random.fold_in(key, 7)
    keys = jax.random.split(key, 5)
    bodies = jnp.arange(BODIES, dtype=jnp.int32)[:, None]
    spread = 3 * TGT_BODIES
    column = jnp.arange(spread, dtype=jnp.int32)[None, :]
    candidate = (bodies // TGT_BODIES - 1) * TGT_BODIES + column
    usable = (candidate >= 0) & (candidate < BODIES) & (candidate != bodies)
    step_x = 7 * (candidate // 2 - bodies // 2)
    step_y = 24 * (candidate % 2 - bodies % 2)
    score = step_x * step_x + step_y * step_y
    jitter = jax.random.randint(keys[0], (BODIES, spread), 0, 64, jnp.int32)
    ranked = jnp.where(usable, score * 64 + jitter, (1 << 30) + column)
    ranking = jnp.argsort(ranked, axis=1, stable=True)[:, :NEAR]
    chosen = jnp.take_along_axis(candidate, ranking, axis=1)
    first_draw = jax.random.randint(keys[1], (BODIES, 1), 0, NEAR, jnp.int32)
    second_draw = jax.random.randint(keys[2], (BODIES, 1), 0, NEAR, jnp.int32)
    counted = jnp.maximum(first_draw, second_draw) + 1
    counted = jnp.where(bodies % 16 == 5, NEAR, counted)
    block_of = bodies // TGT_BODIES
    last_block = BODIES // TGT_BODIES - 1
    coin = jax.random.randint(keys[3], (BODIES, 1), 0, 2, jnp.int32)
    direction = jnp.where(block_of == 0, 1, jnp.where(block_of == last_block, -1, 2 * coin - 1))
    place = jnp.arange(TGT_BODIES, dtype=jnp.int32)[None, :]
    partner = (block_of + direction) * TGT_BODIES + place
    reach = jnp.abs(partner - bodies)
    taken = jnp.any(partner[:, :, None] == chosen[:, None, :], axis=2)
    eligible = (reach >= max(TGT_BODIES // 2, 1)) & jnp.logical_not(taken)
    far_jitter = jax.random.randint(keys[4], (BODIES, TGT_BODIES), 0, 1 << 16, jnp.int32)
    far_score = jnp.where(eligible, far_jitter * TGT_BODIES + place + 1, 0)
    far_rank = jnp.argsort(-far_score, axis=1, stable=True)[:, :1]
    far_pick = jnp.take_along_axis(partner, far_rank, axis=1)
    has_far = jnp.any(eligible, axis=1, keepdims=True)
    slots = jnp.arange(NEAR, dtype=jnp.int32)[None, :]
    result = jnp.where(slots < counted, chosen, -1)
    result = jnp.where((slots == counted - 1) & has_far, far_pick, result)
    return result.astype(jnp.int32)


def block_scale(stream_key, shape, cuts, least, largest):
    def one(dim, shards_of):
        heights = jax.random.uniform(jax.random.fold_in(jax.random.fold_in(stream_key, 6), dim), (shards_of,), jnp.float32, least / len(cuts), largest / len(cuts))
        return jnp.repeat(jnp.exp(heights), shape[dim] // shards_of).reshape((-1,) + (1,) * (len(shape) - dim - 1))

    loudness = one(*cuts[0])
    for cut in cuts[1:]:
        loudness = loudness * one(*cut)
    return loudness


def centred(stream_key, extent, scale, bound, cuts=(), kind=jnp.bfloat16):
    values = scale * jax.random.normal(stream_key, extent, jnp.float32)
    if cuts:
        values = values * block_scale(stream_key, extent, cuts, -0.22, 0.18)
    return jnp.clip(values, -bound, bound).astype(kind)


def setup_inputs(seed: int = 0) -> dict:
    streams_of = jax.random.split(jax.random.key(seed), 8)
    positions = draw_positions(jax.random.fold_in(streams_of[7], 71), 0)
    weights = jnp.clip(jnp.exp(math.log(0.062305298) - 2.3025852 * jax.random.uniform(streams_of[1], (BODIES, P_SIZE), jnp.float32) ** block_scale(streams_of[1], (BODIES, P_SIZE), ((0, 256),), -0.2, 0.2)), 0.0062305294, 0.062305298)
    density = centred(streams_of[2], (BODIES, 3, P_SIZE), 1.0, 6.0, ((0, 256),), jnp.float32)
    near_source = draw_near_source(jax.random.fold_in(streams_of[7], 71), 0)
    couplings = centred(streams_of[4], (BODIES, BODIES, RANK, RANK), (BODIES * RANK) ** -0.5, 0.046875, ((0, 32), (1, 8)))
    source_basis = centred(streams_of[5], (BODIES, RANK, 3, P_SIZE), (3 * P_SIZE) ** -0.5, 0.125, ((0, 256),))
    target_basis = centred(streams_of[6], (BODIES, RANK, 3, P_SIZE), RANK ** -0.5, 1.5, ((0, 256),))
    return dict(positions=positions, weights=weights, density=density, near_source=near_source, couplings=couplings, source_basis=source_basis, target_basis=target_basis)


def stokeslet(target, source):
    weighted = source[3:6] * source[6:7]
    delta_x = target[0][:, None] - source[0][None, :]
    delta_y = target[1][:, None] - source[1][None, :]
    delta_z = target[2][:, None] - source[2][None, :]
    squared = delta_x * delta_x + delta_y * delta_y + delta_z * delta_z
    inverse = 1.0 / jnp.sqrt(squared)
    cubed = inverse * inverse * inverse
    along = delta_x * weighted[0][None, :] + delta_y * weighted[1][None, :] + delta_z * weighted[2][None, :]
    pull = along * cubed
    first = lax.optimization_barrier(jnp.sum(weighted[0][None, :] * inverse + delta_x * pull, axis=1))
    second = lax.optimization_barrier(jnp.sum(weighted[1][None, :] * inverse + delta_y * pull, axis=1))
    third = lax.optimization_barrier(jnp.sum(weighted[2][None, :] * inverse + delta_z * pull, axis=1))
    return jnp.stack([first, second, third], 0)

def reference(positions, weights, density, near_source, couplings, source_basis, target_basis):
    highest = lax.Precision.HIGHEST
    coef = jnp.einsum('brcp,bcp->br', source_basis.astype(jnp.float32), density, precision=highest).astype(jnp.bfloat16)
    coef_wide = coef.astype(jnp.float32)
    every = jnp.arange(BODIES, dtype=jnp.int32)

    def far_rows(start):
        block = lax.dynamic_slice_in_dim(couplings, start, TGT_BODIES, 0).astype(jnp.float32)
        lists = lax.dynamic_slice_in_dim(near_source, start, TGT_BODIES, 0)
        listed = jnp.any(lists[:, :, None] == every[None, None, :], axis=1)
        itself = (start + jnp.arange(TGT_BODIES, dtype=jnp.int32))[:, None] == every[None, :]
        keep = jnp.logical_not(jnp.logical_or(listed, itself))
        masked = jnp.where(keep[:, :, None], coef_wide[None, :, :], jnp.float32(0.0))
        return jnp.einsum('ijrs,ijs->ir', block, masked, precision=highest)
    starts = jnp.arange(BODIES // TGT_BODIES, dtype=jnp.int32) * TGT_BODIES
    coupled = lax.map(far_rows, starts).reshape(BODIES, RANK).astype(jnp.bfloat16)
    far_velocity = jnp.einsum('brcp,br->bcp', target_basis.astype(jnp.float32), coupled.astype(jnp.float32), precision=highest)
    packed = jnp.concatenate([positions, density, weights[:, None, :]], axis=1)

    def near_body(index):
        listed = near_source[index]
        active = listed >= 0
        chosen = jnp.where(active, listed, 0).astype(jnp.int32)
        sources = packed[chosen]
        values = jax.vmap(stokeslet, in_axes=(None, 0))(positions[index], sources)
        values = jnp.where(active[:, None, None], values, jnp.float32(0.0))
        return lax.optimization_barrier(jnp.sum(values, axis=0))
    near_velocity = lax.map(near_body, every)
    return far_velocity + near_velocity
```

```python
import functools
import jax
import jax.numpy as jnp
from jax import lax
from jax.experimental import pallas as pl
from jax.experimental.pallas import tpu as pltpu
from jax.sharding import PartitionSpec as P

F32 = jnp.float32
BF16 = jnp.bfloat16
LANES = 768
ROWS = 656
MAIN = 640
COMPS = 6
FAR_AWAY = 1000.0
LEAST_GAP = 0.1
MOST_RATIO = 70.0
MESH = pl.DeviceIdType.MESH


def remote(source, target, send, recv, device):
    return pltpu.make_async_remote_copy(
        src_ref=source,
        dst_ref=target,
        send_sem=send,
        recv_sem=recv,
        device_id=device,
        device_id_type=MESH,
    )


def exchange_kernel(
    nodes,
    positions,
    weights,
    density,
    near,
    couplings,
    basis,
    geometry,
    coupled,
    held,
    coef_mine,
    coef_relay,
    coef_sum,
    coef_parts,
    lists,
    mask,
    folded,
    far_mine,
    far_parts,
    held_sem,
    list_send,
    list_recv,
    first_send,
    first_recv,
    second_send,
    second_recv,
    far_send,
    far_recv,
    row_send,
    row_recv,
    halo_send,
    halo_recv,
):
    t = lax.axis_index("tgt")
    s = lax.axis_index("src")
    t_count = lax.axis_size("tgt")
    x = s // 2
    z = s % 2
    group = t // 8
    place = t % 8
    quarter = t // 4
    own = positions.shape[1]
    loops_back = jnp.logical_and(quarter == s, place == s)

    load = pltpu.make_async_copy(couplings, held, held_sem)
    load.start()

    barrier = pltpu.get_barrier_semaphore()

    def greet(device):
        pl.semaphore_signal(barrier, inc=1, device_id=device, device_id_type=MESH)

    for step in range(1, 8):
        greet((t, (s + step) % 8))
        greet((group * 8 + (place + step) % 8, s))
    for part in range(4):

        @pl.when(jnp.logical_not(jnp.logical_and(loops_back, part == t % 4)))
        def _():
            greet((4 * s + part, place))

    @pl.when(t > 0)
    def _():
        greet((t - 1, s))

    @pl.when(t < t_count - 1)
    def _():
        greet((t + 1, s))

    def block(row, column):
        return geometry.at[pl.ds((row * 8 + column) * COMPS, COMPS)]

    base = (8 + s) * COMPS
    pad = jnp.zeros((own, LANES - nodes), F32)
    for c in range(3):
        geometry[base + c] = jnp.concatenate([positions[c], pad + FAR_AWAY], axis=1)
        geometry[base + 3 + c] = jnp.concatenate([density[c] * weights[...], pad], axis=1)
    lists[s] = jnp.concatenate([near[...], jnp.full((own, 120), -1, jnp.int32)], axis=1)

    lane = lax.broadcasted_iota(jnp.int32, (16, 128), 1)
    spread = jnp.zeros((16, 128), F32)
    for j in range(own):
        product = basis[j, 0].astype(F32) * density[0, j : j + 1, :]
        for c in range(1, 3):
            product = product + basis[j, c].astype(F32) * density[c, j : j + 1, :]
        value = jnp.sum(product, axis=1, keepdims=True)
        spread = jnp.where(lane == (t % 4) * 32 + s * 4 + j, value, spread)
    coef_mine[...] = spread.astype(BF16)

    pl.semaphore_wait(
        barrier,
        7
        + 7
        + jnp.where(loops_back, 3, 4)
        + jnp.where(t > 0, 1, 0)
        + jnp.where(t < t_count - 1, 1, 0),
    )

    started = []

    def first_copy(u):
        return remote(
            coef_mine,
            coef_relay.at[t % 4],
            first_send.at[u],
            first_recv.at[t % 4],
            (u * 8 + s, quarter),
        )

    for u in range(4):
        away = jnp.logical_not(jnp.logical_and(loops_back, u == group))

        @pl.when(away)
        def _():
            first_copy(u).start()

        @pl.when(jnp.logical_not(away))
        def _():
            coef_relay[t % 4] = coef_mine[...]

    def row_copy(index, column, device):
        return remote(
            block(1, column),
            block(1, column),
            row_send.at[index],
            row_recv.at[index],
            device,
        )

    def right(column):
        return (column + 2) % 8

    def left(column):
        return (column + 6) % 8

    def halo_copy(side, index, column):
        return remote(
            block(1, column),
            block(2 * side, column),
            halo_send.at[side * 8 + index],
            halo_recv.at[side * 8 + index],
            (t + 1 - 2 * side, s),
        )

    def halo_start(index, column):
        @pl.when(t < t_count - 1)
        def _():
            halo_copy(0, index, column).start()

        @pl.when(t > 0)
        def _():
            halo_copy(1, index, column).start()

    partner = s + 1 - 2 * z
    copies = {}

    def row_start(index, column, device):
        copies[index] = row_copy(index, column, device)
        copies[index].start()

    def ring_start(turn, column):
        row_start(1 + 3 * turn, column, (t, right(s)))
        row_start(2 + 3 * turn, column, (t, left(s)))
        halo_start(4 * turn, column)

    def ring_forward(turn, column):
        copies[1 + 3 * turn].wait_recv()
        copies[2 + 3 * turn].wait_recv()
        even = t % 2 == 0
        from_left = left(column)
        from_right = right(column)
        passed = jnp.where(even, from_left, from_right)
        row_start(3 + 3 * turn, passed, (t, jnp.where(even, right(s), left(s))))
        halo_start(4 * turn + 1, from_left)
        halo_start(4 * turn + 2, from_right)

    def ring_end(turn, column):
        copies[3 + 3 * turn].wait_recv()
        halo_start(4 * turn + 3, (column + 4) % 8)

    row_start(0, s, (t, partner))
    ring_start(0, s)

    def list_copy(step):
        return remote(
            lists.at[s],
            lists.at[s],
            list_send.at[step - 1],
            list_recv.at[step - 1],
            (t, (s + step) % 8),
        )

    list_copies = [list_copy(step) for step in range(1, 8)]
    for copy in list_copies:
        copy.start()

    for part in range(4):

        @pl.when(jnp.logical_not(jnp.logical_and(loops_back, part == t % 4)))
        def _():
            remote(
                coef_mine,
                coef_relay.at[part],
                first_send.at[part],
                first_recv.at[part],
                (4 * s + part, place),
            ).wait_recv()

    total = coef_relay[0].astype(F32)
    for part in range(1, 4):
        total = total + coef_relay[part].astype(F32)
    coef_sum[...] = total.astype(BF16)
    second_copies = []
    for step in range(1, 8):
        copy = remote(
            coef_sum,
            coef_parts.at[step - 1],
            second_send.at[step - 1],
            second_recv.at[step - 1],
            (group * 8 + (place + step) % 8, s),
        )
        copy.start()
        second_copies.append(copy)

    ring_forward(0, s)
    copies[0].wait_recv()
    ring_start(1, partner)

    for copy in list_copies:
        copy.wait_recv()
    rows = 8 * own
    listed = lists[...].reshape(rows, 128)
    ids = s * 128 + lax.broadcasted_iota(jnp.int32, (rows, 128), 1)
    hit = ids == t * rows + lax.broadcasted_iota(jnp.int32, (rows, 128), 0)
    for k in range(near.shape[1]):
        hit = jnp.logical_or(hit, ids == listed[:, k : k + 1])
    mask[...] = jnp.where(hit, F32(0.0), F32(1.0))
    for copy in second_copies:
        copy.wait_recv()
    coef = coef_sum[...].astype(F32)
    for step in range(1, 8):
        coef = coef + coef_parts[step - 1].astype(F32)
    load.wait()

    def fold(i, _):
        kept = coef * mask[pl.ds(i, 1), :]
        product = held[i].astype(F32) * kept[None]
        folded[pl.ds(pl.multiple_of(i * 16, 16), 16), :] = jnp.sum(product, axis=1)
        return 0

    lax.fori_loop(0, rows, fold, 0)
    for q in range(4):
        turned = folded[q * 128 : (q + 1) * 128, :].T
        far_mine[q] = jnp.broadcast_to(jnp.sum(turned, axis=0, keepdims=True), (8, 128))
    far_copies = []
    for step in range(1, 8):
        other = (s + step) % 8
        copy = remote(
            far_mine.at[other // 2],
            far_parts.at[step - 1],
            far_send.at[step - 1],
            far_recv.at[step - 1],
            (t, other),
        )
        copy.start()
        far_copies.append(copy)

    ring_end(0, s)
    ring_forward(1, partner)
    ring_end(1, partner)

    for copy in far_copies:
        copy.wait_recv()
    w = far_mine[s // 2]
    for step in range(1, 8):
        w = w + far_parts[step - 1]
    coupled[...] = jnp.where(s % 2 == 1, pltpu.roll(w, 64, 1), w)

    for side in range(2):
        there = t > 0 if side == 0 else t < t_count - 1
        mine = t < t_count - 1 if side == 0 else t > 0

        @pl.when(there)
        def _():
            for index in range(8):
                start = s if index < 4 else partner
                column = (start + (0, 6, 2, 4)[index % 4]) % 8
                remote(
                    block(1, column),
                    block(2 * side, column),
                    halo_send.at[side * 8 + index],
                    halo_recv.at[side * 8 + index],
                    (t, s),
                ).wait_recv()

        @pl.when(mine)
        def _():
            for index in range(8):
                start = s if index < 4 else partner
                halo_copy(side, index, (start + (0, 6, 2, 4)[index % 4]) % 8).wait_send()

    for copy in list_copies + second_copies + far_copies + list(copies.values()):
        copy.wait_send()
    for u in range(4):

        @pl.when(jnp.logical_not(jnp.logical_and(loops_back, u == group)))
        def _():
            first_copy(u).wait_send()


def split(value):
    high = value.astype(BF16).astype(F32)
    rest = value - high
    middle = rest.astype(BF16).astype(F32)
    return high, middle, rest - middle


def velocity_kernel(
    nodes,
    near,
    geometry,
    coupled,
    basis,
    out,
    used,
    centre,
    features,
    spread0,
    spread1,
    moment0,
    moment1,
    kernel0,
    kernel1,
    total,
    slots,
    worst,
    columns,
):
    t = lax.axis_index("tgt")
    s = lax.axis_index("src")
    own = out.shape[1]
    per_body = near.shape[1]
    first_id = (t - 1) * 32
    own_base = (8 + s) * COMPS
    total[...] = jnp.zeros_like(total)
    moment1[...] = jnp.zeros_like(moment1)
    kernel1[...] = jnp.zeros_like(kernel1)
    worst[...] = jnp.full_like(worst, -1.0)
    for i in range(own):
        for c in range(COMPS):
            slots[i * COMPS + c] = jnp.full((8, LANES), FAR_AWAY if c < 3 else 0.0, F32)

    def listing(k, n):
        active = near[k // per_body, k % per_body] >= 0

        @pl.when(active)
        def _():
            used[n] = k

        return n + jnp.where(active, 1, 0)

    n = lax.fori_loop(0, own * per_body, listing, jnp.int32(0))
    used[n] = 0
    used[n + 1] = 0

    inside = lax.broadcasted_iota(jnp.int32, (own, LANES), 1) < nodes
    radius = jnp.zeros((own, LANES), F32)
    for c in range(3):
        value = geometry[own_base + c]
        mean = jnp.sum(jnp.where(inside, value, 0.0), axis=1, keepdims=True) / nodes
        centre[c] = jnp.broadcast_to(mean, (own, LANES))
        offset = jnp.where(inside, value - mean, 0.0)
        radius = radius + offset * offset
    largest = jnp.max(radius, axis=1, keepdims=True)
    centre[3] = jnp.broadcast_to(jnp.sqrt(largest), (own, LANES))

    def target_rows(i):
        return [geometry[own_base + c, i : i + 1, :] - centre[c, i : i + 1, :] for c in range(3)]

    for i in range(own):
        x = target_rows(i)
        square = x[0] * x[0] + x[1] * x[1] + x[2] * x[2]
        one = jnp.ones_like(square)
        zero = jnp.zeros_like(square)
        parts = split(jnp.concatenate(x + [one, square, zero, zero, zero], axis=0))
        empty = jnp.zeros((8, LANES), F32)
        stack = []
        for part in parts:
            stack += [part, part, part, empty]
        features[i] = jnp.concatenate(stack, axis=0).astype(BF16)[:, :MAIN]

    sub = lax.broadcasted_iota(jnp.int32, (8, LANES), 0)

    def pair(m):
        k = used[m]
        body = near[k // per_body, k % per_body] - first_id
        return k // per_body, k % per_body, (body // 4) * COMPS, body % 4

    def source_stage(m, spread, moment):
        i, slot, base, place = pair(m)
        raw = [geometry[base + c, pl.ds(place, 1), :] for c in range(COMPS)]
        live = jnp.where(m < n, F32(1.0), F32(0.0))

        for c in range(COMPS):
            slots[i * COMPS + c, pl.ds(slot, 1), :] = raw[c]

        y = [
            jnp.broadcast_to(raw[c] - centre[c, pl.ds(i, 1), :], (8, LANES)) for c in range(3)
        ]
        w = [jnp.broadcast_to(raw[3 + c], (8, LANES)) for c in range(3)]
        square = y[0] * y[0] + y[1] * y[1] + y[2] * y[2]
        reach = jnp.sqrt(square)
        size = jnp.broadcast_to(centre[3, pl.ds(i, 1), :], (8, LANES))
        ratio = (reach + size) - MOST_RATIO * jnp.maximum(reach - size, LEAST_GAP)
        worst[...] = jnp.maximum(worst[...], ratio)
        along = y[0] * w[0] + y[1] * w[1] + y[2] * w[2]
        left = jnp.where(
            sub == 0,
            -2.0 * y[0],
            jnp.where(
                sub == 1,
                -2.0 * y[1],
                jnp.where(
                    sub == 2,
                    -2.0 * y[2],
                    jnp.where(sub == 3, square, jnp.where(sub == 4, F32(1.0), F32(0.0))),
                ),
            ),
        )
        empty = jnp.zeros((8, LANES), F32)
        third = jnp.concatenate(list(split(left)) + [empty], axis=0).astype(BF16)[:, :ROWS]
        spread[...] = jnp.concatenate([third, third, third], axis=0)
        quad = sub % 4
        plain = live * jnp.where(
            quad == 0, w[0], jnp.where(quad == 1, w[1], jnp.where(quad == 2, w[2], along))
        )
        once = plain * jnp.where(sub < 4, y[0], y[1])
        twice = plain * jnp.where(sub < 4, y[2], square)
        parts = [split(value) for value in (plain, once, twice)]
        stack = [parts[q][p] for p in range(3) for q in range(3)] + [empty]
        moment[...] = jnp.concatenate(stack, axis=0).astype(BF16)[:, :ROWS]

    def kernel_chunk(m, spread, kernel, low, high):
        i = used[m] // per_body
        squared = lax.dot_general(
            spread[:, low:high],
            features[i],
            (((0,), (0,)), ((), ())),
            preferred_element_type=F32,
        )
        inverse = lax.rsqrt(squared)
        kernel[low:high] = (inverse * inverse * inverse).astype(BF16)

    def moment_chunk(m, kernel, moment, low, high):
        i = used[jnp.maximum(m, 0)] // per_body
        total[i] += jnp.dot(moment[:, low:high], kernel[low:high], preferred_element_type=F32)

    cuts = (0, 208, 432, ROWS)

    def turn(q, _):
        first = (kernel0, moment0, spread0)
        second = (kernel1, moment1, spread1)
        for e, (mine, other) in enumerate(((first, second), (second, first))):
            m = 2 * q + e
            for low, high in zip(cuts[:-1], cuts[1:]):
                kernel_chunk(m, mine[2], mine[0], low, high)
                moment_chunk(m - 1, other[0], other[1], low, high)
            source_stage(m + 1, other[2], other[1])
        return 0

    halves = (n + 1) // 2
    source_stage(0, spread0, moment0)
    lax.fori_loop(0, halves, turn, 0)
    moment_chunk(2 * halves - 1, kernel1, moment1, 0, ROWS)

    row8 = lax.broadcasted_iota(jnp.int32, (8, 128), 0)
    lane8 = lax.broadcasted_iota(jnp.int32, (8, 128), 1)
    diagonal = jnp.where(lane8 // 16 == row8, coupled[...], 0.0).astype(BF16)[:, :64]
    far = []
    for c in range(3):
        flat = jnp.concatenate([basis[i, c] for i in range(own)], axis=0)
        far.append(jnp.dot(diagonal, flat, preferred_element_type=F32))

    for i in range(own):
        y = [slots[i * COMPS + c] for c in range(3)]
        w = [slots[i * COMPS + 3 + c] for c in range(3)]
        sums = [[], [], []]
        for node in range(MAIN, nodes):
            d = [geometry[own_base + c, i : i + 1, node : node + 1] - y[c] for c in range(3)]
            inverse = lax.rsqrt(d[0] * d[0] + d[1] * d[1] + d[2] * d[2])
            pull = (d[0] * w[0] + d[1] * w[1] + d[2] * w[2]) * (inverse * inverse * inverse)
            for c in range(3):
                value = w[c] * inverse + d[c] * pull
                folded = jnp.sum(value, axis=0, keepdims=True)
                sums[c].append(jnp.sum(folded, axis=1, keepdims=True))
        for c in range(3):
            tail = jnp.concatenate(sums[c], axis=1)
            out[c, i : i + 1, MAIN:nodes] = tail + far[c][i : i + 1, MAIN:nodes]

    crowded = jnp.max(worst[...]) > 0.0

    @pl.when(jnp.logical_not(crowded))
    def _():
        for i in range(own):
            at = total[i]
            g = at[0:24] + at[24:48] + at[48:72]
            x = [value[:, :MAIN] for value in target_rows(i)]
            plain = [g[k : k + 1] for k in range(3)]
            first = [[g[b + k : b + k + 1] for k in range(3)] for b in (8, 12, 16)]
            along = [g[b + 3 : b + 4] for b in (3 - 3, 8, 12, 16)]
            second = [g[20 + k : 21 + k] for k in range(3)]
            square = x[0] * x[0] + x[1] * x[1] + x[2] * x[2]
            inner = x[0] * plain[0] + x[1] * plain[1] + x[2] * plain[2] - along[0]
            for c in range(3):
                u = square * plain[c] + second[c] + along[1 + c] + x[c] * inner
                for k in range(3):
                    u = u - x[k] * (2.0 * first[k][c] + first[c][k])
                out[c, i : i + 1, :MAIN] = u + far[c][i : i + 1, :MAIN]

    @pl.when(crowded)
    def _():
        for i in range(own):
            for c in range(3):
                out[c, i : i + 1, :MAIN] = far[c][i : i + 1, :MAIN]

        def direct(m, _):
            i, slot, base, place = pair(m)
            rows = [geometry[base + c, pl.ds(place, 1), :] for c in range(COMPS)]
            empty = jnp.zeros((2, LANES), F32)
            columns[...] = jnp.concatenate(rows + [empty], axis=0).T
            x = [geometry[own_base + c, pl.ds(i, 1), :MAIN] for c in range(3)]

            def eight(q, sums):
                block = columns[pl.ds(pl.multiple_of(q * 8, 8), 8), :]
                d = [x[c] - block[:, c : c + 1] for c in range(3)]
                w = [block[:, 3 + c : 4 + c] for c in range(3)]
                inverse = lax.rsqrt(d[0] * d[0] + d[1] * d[1] + d[2] * d[2])
                pull = d[0] * w[0] + d[1] * w[1] + d[2] * w[2]
                pull = pull * (inverse * inverse * inverse)
                return tuple(sums[c] + (w[c] * inverse + d[c] * pull) for c in range(3))

            start = tuple(jnp.zeros((8, MAIN), F32) for _ in range(3))
            sums = lax.fori_loop(0, ROWS // 8, eight, start)
            for c in range(3):
                out[c, pl.ds(i, 1), :MAIN] += jnp.sum(sums[c], axis=0, keepdims=True)
            return 0

        lax.fori_loop(0, n, direct, 0)


def local(positions, weights, density, near_source, couplings, source_basis, target_basis):
    own, _, nodes = positions.shape
    vmem = pl.BlockSpec(memory_space=pltpu.VMEM)
    dma = pltpu.SemaphoreType.DMA
    turned = (1, 0, 2)
    geometry, coupled = pl.pallas_call(
        functools.partial(exchange_kernel, nodes),
        out_shape=(
            jax.ShapeDtypeStruct((24 * COMPS, own, LANES), F32),
            jax.ShapeDtypeStruct((8, 128), F32),
        ),
        in_specs=[vmem] * 4 + [pl.BlockSpec(memory_space=pl.ANY), vmem],
        out_specs=(vmem, vmem),
        scratch_shapes=[
            pltpu.VMEM((32, 16, 16, 128), BF16),
            pltpu.VMEM((16, 128), BF16),
            pltpu.VMEM((4, 16, 128), BF16),
            pltpu.VMEM((16, 128), BF16),
            pltpu.VMEM((7, 16, 128), BF16),
            pltpu.VMEM((8, own, 128), jnp.int32),
            pltpu.VMEM((32, 128), F32),
            pltpu.VMEM((512, 128), F32),
            pltpu.VMEM((4, 8, 128), F32),
            pltpu.VMEM((7, 8, 128), F32),
            dma,
            dma((7,)),
            dma((7,)),
            dma((4,)),
            dma((4,)),
            dma((7,)),
            dma((7,)),
            dma((7,)),
            dma((7,)),
            dma((7,)),
            dma((7,)),
            dma((16,)),
            dma((16,)),
        ],
        compiler_params=pltpu.CompilerParams(
            collective_id=0, has_side_effects=True, vmem_limit_bytes=32 * 2**20
        ),
        name="exchange",
    )(
        positions.transpose(turned),
        weights,
        density.transpose(turned),
        near_source,
        couplings.transpose(0, 2, 3, 1),
        source_basis.transpose(0, 2, 1, 3),
    )
    out = pl.pallas_call(
        functools.partial(velocity_kernel, nodes),
        out_shape=jax.ShapeDtypeStruct((3, own, nodes), F32),
        in_specs=[pl.BlockSpec(memory_space=pltpu.SMEM)] + [vmem] * 3,
        out_specs=vmem,
        scratch_shapes=[
            pltpu.SMEM((40,), jnp.int32),
            pltpu.VMEM((4, own, LANES), F32),
            pltpu.VMEM((own, 96, MAIN), BF16),
            pltpu.VMEM((96, ROWS), BF16),
            pltpu.VMEM((96, ROWS), BF16),
            pltpu.VMEM((80, ROWS), BF16),
            pltpu.VMEM((80, ROWS), BF16),
            pltpu.VMEM((ROWS, MAIN), BF16),
            pltpu.VMEM((ROWS, MAIN), BF16),
            pltpu.VMEM((own, 80, MAIN), F32),
            pltpu.VMEM((own * COMPS, 8, LANES), F32),
            pltpu.VMEM((8, LANES), F32),
            pltpu.VMEM((LANES, 8), F32),
        ],
        compiler_params=pltpu.CompilerParams(vmem_limit_bytes=32 * 2**20),
        name="velocity",
    )(near_source, geometry, coupled, target_basis.transpose(0, 2, 1, 3))
    return out.transpose(turned)


def solution(mesh):
    placed = (
        P(("tgt", "src"), None, None),
        P(("tgt", "src"), None),
        P(("tgt", "src"), None, None),
        P(("tgt", "src"), None),
        P("tgt", "src", None, None),
        P(("tgt", "src"), None, None, None),
        P(("tgt", "src"), None, None, None),
    )
    return jax.shard_map(
        local, mesh=mesh, in_specs=placed, out_specs=P(("tgt", "src"), None, None), check_vma=False
    )
```

```python
import functools
import jax
import jax.numpy as jnp
from jax import lax
from jax.experimental import pallas as pl
from jax.experimental.pallas import tpu as pltpu
from jax.sharding import PartitionSpec as P

F32 = jnp.float32
BF16 = jnp.bfloat16
LANES = 768
ROWS = 656
MAIN = 640
COMPS = 6
FAR_AWAY = 1000.0
LEAST_GAP = 0.1
MOST_RATIO = 70.0
EARLY = 3
CUTS = (0, 208, 432, ROWS)
VMEM_BYTES = 58 * 2**20
MESH = pl.DeviceIdType.MESH


def remote(source, target, send, recv, device):
    return pltpu.make_async_remote_copy(
        src_ref=source,
        dst_ref=target,
        send_sem=send,
        recv_sem=recv,
        device_id=device,
        device_id_type=MESH,
    )


def split(value):
    high = value.astype(BF16).astype(F32)
    rest = value - high
    middle = rest.astype(BF16).astype(F32)
    return high, middle, rest - middle


def target_stage(nodes, own, load, centre, features):
    inside = lax.broadcasted_iota(jnp.int32, (own, LANES), 1) < nodes
    radius = jnp.zeros((own, LANES), F32)
    offsets = []
    for c in range(3):
        value = load(c)
        mean = jnp.sum(jnp.where(inside, value, 0.0), axis=1, keepdims=True) / nodes
        centre[c] = jnp.broadcast_to(mean, (own, LANES))
        offset = jnp.where(inside, value - mean, 0.0)
        offsets.append(offset)
        radius = radius + offset * offset
    largest = jnp.max(radius, axis=1, keepdims=True)
    centre[3] = jnp.broadcast_to(jnp.sqrt(largest), (own, LANES))
    for i in range(own):
        x = [offset[i : i + 1, :] for offset in offsets]
        square = radius[i : i + 1, :]
        one = jnp.ones_like(square)
        zero = jnp.zeros_like(square)
        parts = split(jnp.concatenate(x + [one, square, zero, zero, zero], axis=0))
        empty = jnp.zeros((8, LANES), F32)
        stack = []
        for part in parts:
            stack += [part, part, part, empty]
        features[i] = jnp.concatenate(stack, axis=0).astype(BF16)[:, :MAIN]


def source_stage(raw, i, live, centre, worst, spread, moment):
    sub = lax.broadcasted_iota(jnp.int32, (8, LANES), 0)
    y = [jnp.broadcast_to(raw[c] - centre[c, pl.ds(i, 1), :], (8, LANES)) for c in range(3)]
    w = [jnp.broadcast_to(raw[3 + c], (8, LANES)) for c in range(3)]
    square = y[0] * y[0] + y[1] * y[1] + y[2] * y[2]
    reach = jnp.sqrt(square)
    size = jnp.broadcast_to(centre[3, pl.ds(i, 1), :], (8, LANES))
    ratio = (reach + size) - MOST_RATIO * jnp.maximum(reach - size, LEAST_GAP)
    worst[...] = jnp.maximum(worst[...], ratio)
    along = y[0] * w[0] + y[1] * w[1] + y[2] * w[2]
    left = jnp.where(
        sub == 0,
        -2.0 * y[0],
        jnp.where(
            sub == 1,
            -2.0 * y[1],
            jnp.where(
                sub == 2,
                -2.0 * y[2],
                jnp.where(sub == 3, square, jnp.where(sub == 4, F32(1.0), F32(0.0))),
            ),
        ),
    )
    empty = jnp.zeros((8, LANES), F32)
    third = jnp.concatenate(list(split(left)) + [empty], axis=0).astype(BF16)[:, :ROWS]
    spread[...] = jnp.concatenate([third, third, third], axis=0)
    quad = sub % 4
    plain = live * jnp.where(
        quad == 0, w[0], jnp.where(quad == 1, w[1], jnp.where(quad == 2, w[2], along))
    )
    once = plain * jnp.where(sub < 4, y[0], y[1])
    twice = plain * jnp.where(sub < 4, y[2], square)
    parts = [split(value) for value in (plain, once, twice)]
    stack = [parts[q][p] for p in range(3) for q in range(3)] + [empty]
    moment[...] = jnp.concatenate(stack, axis=0).astype(BF16)[:, :ROWS]


def kernel_chunk(features, spread, kernel, low, high):
    squared = lax.dot_general(
        spread[:, low:high], features, (((0,), (0,)), ((), ())), preferred_element_type=F32
    )
    inverse = lax.rsqrt(squared)
    kernel[low:high] = (inverse * inverse * inverse).astype(BF16)


def moment_chunk(kernel, moment, low, high):
    return jnp.dot(moment[:, low:high], kernel[low:high], preferred_element_type=F32)


def near_pairs(count, target_of, source, features, total, first, second):
    def turn(q, _):
        for e, (mine, other) in enumerate(((first, second), (second, first))):
            m = 2 * q + e
            for low, high in zip(CUTS[:-1], CUTS[1:]):
                kernel_chunk(features[target_of(m)], mine[2], mine[0], low, high)
                total[target_of(m - 1)] += moment_chunk(other[0], other[1], low, high)
            source(m + 1, other[2], other[1])
        return 0

    halves = (count + 1) // 2
    source(0, first[2], first[1])
    lax.fori_loop(0, halves, turn, 0)
    total[target_of(2 * halves - 1)] += moment_chunk(second[0], second[1], 0, ROWS)


def exchange_kernel(
    nodes,
    positions_in,
    weights_in,
    density_in,
    near_in,
    couplings_in,
    basis_in,
    row_out,
    halo_out,
    coupled_out,
    total_out,
    worst_out,
    slots_out,
    row_geometry,
    coupled,
    total,
    worst,
    slots,
    positions,
    weights,
    density,
    near,
    near_scalar,
    held,
    basis,
    coef_mine,
    coef_parts,
    lists,
    mask,
    folded,
    far_mine,
    far_parts,
    chosen,
    centre,
    features,
    spread0,
    spread1,
    moment0,
    moment1,
    kernel0,
    kernel1,
    load_sem,
    store_sem,
    list_send,
    list_recv,
    coef_send,
    coef_recv,
    far_send,
    far_recv,
    row_send,
    row_recv,
    halo_send,
    halo_recv,
):
    t = lax.axis_index("tgt")
    s = lax.axis_index("src")
    t_count = lax.axis_size("tgt")
    quarter = t // 4
    own = positions.shape[1]
    slot_count = near.shape[1]
    loops_back = quarter == s
    partner = s + 1 - 2 * (s % 2)

    loads = [
        pltpu.make_async_copy(source, target, load_sem.at[index])
        for index, (source, target) in enumerate(
            (
                (positions_in, positions),
                (weights_in, weights),
                (density_in, density),
                (near_in, near),
                (near_in, near_scalar),
                (basis_in, basis),
                (couplings_in, held),
            )
        )
    ]
    for load in loads:
        load.start()

    barrier = pltpu.get_barrier_semaphore()

    def greet(device):
        pl.semaphore_signal(barrier, inc=1, device_id=device, device_id_type=MESH)

    for step in range(1, 8):
        greet((t, (s + step) % 8))

    def greet_source(k, _):
        @pl.when(jnp.logical_not(jnp.logical_and(loops_back, k == (t % 4) * 8 + s)))
        def _():
            greet((4 * s + k // 8, k % 8))

        return 0

    lax.fori_loop(0, t_count, greet_source, 0)

    @pl.when(t > 0)
    def _():
        greet((t - 1, s))

    @pl.when(t < t_count - 1)
    def _():
        greet((t + 1, s))

    def block(column):
        return row_geometry.at[pl.ds(column * COMPS, COMPS)]

    for load in loads[:4]:
        load.wait()
    pad = jnp.zeros((own, LANES - nodes), F32)
    for c in range(3):
        row_geometry[s * COMPS + c] = jnp.concatenate([positions[c], pad + FAR_AWAY], axis=1)
        row_geometry[s * COMPS + 3 + c] = jnp.concatenate(
            [density[c] * weights[...], pad], axis=1
        )
    lists[s] = jnp.concatenate([near[...], jnp.full((own, 120), -1, jnp.int32)], axis=1)

    loads[5].wait()
    lane = lax.broadcasted_iota(jnp.int32, (16, 128), 1)
    spread = jnp.zeros((16, 128), F32)
    for j in range(own):
        product = basis[j, 0].astype(F32) * density[0, j : j + 1, :]
        for c in range(1, 3):
            product = product + basis[j, c].astype(F32) * density[c, j : j + 1, :]
        value = jnp.sum(product, axis=1, keepdims=True)
        spread = jnp.where(lane == (t % 4) * 32 + s * 4 + j, value, spread)
    coef_mine[...] = spread.astype(BF16)

    pl.semaphore_wait(
        barrier,
        7
        + t_count
        - jnp.where(loops_back, 1, 0)
        + jnp.where(t > 0, 1, 0)
        + jnp.where(t < t_count - 1, 1, 0),
    )

    def row_copy(index, column, device):
        return remote(
            block(column), block(column), row_send.at[index], row_recv.at[index], (t, device)
        )

    def halo_copy(side, index, column):
        return remote(
            block(column),
            halo_out.at[pl.ds((side * 8 + column) * COMPS, COMPS)],
            halo_send.at[side * 8 + index],
            halo_recv.at[side * 8 + index],
            (t + 1 - 2 * side, s),
        )

    def halo_start(index, column):
        @pl.when(t < t_count - 1)
        def _():
            halo_copy(0, index, column).start()

        @pl.when(t > 0)
        def _():
            halo_copy(1, index, column).start()

    def across_start(turn, column):
        for step in range(1, 4):
            row_copy(turn * 3 + step, column, (s + 2 * step) % 8).start()
        halo_start(4 * turn, column)

    def across_wait(turn, column):
        for step in range(1, 4):
            here = (column + 8 - 2 * step) % 8
            row_copy(turn * 3 + step, here, partner).wait_recv()
            halo_start(4 * turn + step, here)

    def coef_copy(k):
        return remote(
            coef_mine,
            coef_parts.at[(t % 4) * 8 + s],
            coef_send.at[k],
            coef_recv.at[(t % 4) * 8 + s],
            (k, quarter),
        )

    def away(k):
        return jnp.logical_not(jnp.logical_and(loops_back, k == t))

    def coef_start(k, _):
        @pl.when(away(k))
        def _():
            coef_copy(k).start()

        return 0

    def list_copy(step):
        return remote(
            lists.at[s],
            lists.at[s],
            list_send.at[step - 1],
            list_recv.at[step - 1],
            (t, (s + step) % 8),
        )

    row_copy(0, s, partner).start()
    lax.fori_loop(0, t_count, coef_start, 0)
    across_start(0, s)
    for step in range(1, 8):
        list_copy(step).start()

    @pl.when(loops_back)
    def _():
        coef_parts[(t % 4) * 8 + s] = coef_mine[...]

    loads[4].wait()
    for i in range(own):
        rank = jnp.int32(0)
        picks = [t * 32 + s * 4 + (i + 1) % own] * EARLY
        lives = [jnp.int32(0)] * EARLY
        for k in range(slot_count):
            body = near_scalar[i, k]
            inside = jnp.where(body >= t * 32, 1, 0) * jnp.where(body < t * 32 + 32, 1, 0)
            for e in range(EARLY):
                hit = inside * jnp.where(rank == e, 1, 0)
                picks[e] = jnp.where(hit == 1, body, picks[e])
                lives[e] = lives[e] + hit
            rank = rank + inside
        for e in range(EARLY):
            chosen[2 * (i * EARLY + e)] = picks[e] - t * 32
            chosen[2 * (i * EARLY + e) + 1] = lives[e]

    target_stage(nodes, own, lambda c: row_geometry[s * COMPS + c], centre, features)
    total[...] = jnp.zeros_like(total)
    worst[...] = jnp.full_like(worst, -1.0)
    for k in range(own * COMPS):
        slots[k] = jnp.full((8, LANES), FAR_AWAY if k % COMPS < 3 else 0.0, F32)
    moment1[...] = jnp.zeros_like(moment1)
    kernel1[...] = jnp.zeros_like(kernel1)

    across_wait(0, s)
    row_copy(0, partner, partner).wait_recv()
    across_start(1, partner)

    for step in range(1, 8):
        remote(
            lists.at[s],
            lists.at[(s + 8 - step) % 8],
            list_send.at[step - 1],
            list_recv.at[step - 1],
            (t, partner),
        ).wait_recv()
    rows = 8 * own
    listed = lists[...].reshape(rows, 128)
    ids = s * 128 + lax.broadcasted_iota(jnp.int32, (rows, 128), 1)
    hit = ids == t * rows + lax.broadcasted_iota(jnp.int32, (rows, 128), 0)
    for k in range(slot_count):
        hit = jnp.logical_or(hit, ids == listed[:, k : k + 1])
    mask[...] = jnp.where(hit, F32(0.0), F32(1.0))

    def coef_wait(k, _):
        @pl.when(jnp.logical_not(jnp.logical_and(loops_back, k == (t % 4) * 8 + s)))
        def _():
            remote(
                coef_mine, coef_parts.at[k], coef_send.at[k], coef_recv.at[k], (t, partner)
            ).wait_recv()

        return 0

    lax.fori_loop(0, t_count, coef_wait, 0)
    coef = coef_parts[0].astype(F32)
    for k in range(1, t_count):
        coef = coef + coef_parts[k].astype(F32)
    loads[6].wait()

    def fold(i, _):
        kept = coef * mask[pl.ds(i, 1), :]
        product = held[i].astype(F32) * kept[None]
        folded[pl.ds(pl.multiple_of(i * 16, 16), 16), :] = jnp.sum(product, axis=1)
        return 0

    lax.fori_loop(0, rows, fold, 0)
    for q in range(4):
        turned = folded[q * 128 : (q + 1) * 128, :].T
        far_mine[q] = jnp.broadcast_to(jnp.sum(turned, axis=0, keepdims=True), (8, 128))

    def far_copy(step):
        other = (s + step) % 8
        return remote(
            far_mine.at[other // 2],
            far_parts.at[step - 1],
            far_send.at[step - 1],
            far_recv.at[step - 1],
            (t, other),
        )

    for step in range(1, 8):
        far_copy(step).start()

    across_wait(1, partner)

    def store(index, source, target):
        copy = pltpu.make_async_copy(source, target, store_sem.at[index])
        copy.start()
        return copy

    stores = [store(0, row_geometry, row_out)]

    def source(m, spread, moment):
        now = jnp.minimum(m, own * EARLY - 1)
        i = now // EARLY
        e = now % EARLY
        body = chosen[2 * now]
        live = chosen[2 * now + 1]
        base = (body // 4) * COMPS
        raw = [row_geometry[base + c, pl.ds(body % 4, 1), :] for c in range(COMPS)]
        scale = live.astype(F32) * jnp.where(m < own * EARLY, F32(1.0), F32(0.0))
        for c in range(3):
            slots[i * COMPS + c, pl.ds(e, 1), :] = raw[c]
            slots[i * COMPS + 3 + c, pl.ds(e, 1), :] = raw[3 + c] * live.astype(F32)
        source_stage(raw, i, scale, centre, worst, spread, moment)

    def target_of(m):
        return jnp.clip(m, 0, own * EARLY - 1) // EARLY

    near_pairs(
        own * EARLY,
        target_of,
        source,
        features,
        total,
        (kernel0, moment0, spread0),
        (kernel1, moment1, spread1),
    )
    stores.append(store(1, total, total_out))
    stores.append(store(2, worst, worst_out))
    stores.append(store(3, slots, slots_out))

    for step in range(1, 8):
        far_copy(step).wait_recv()
    w = far_mine[s // 2]
    for step in range(1, 8):
        w = w + far_parts[step - 1]
    coupled[...] = jnp.where(s % 2 == 1, pltpu.roll(w, 64, 1), w)

    stores.append(store(4, coupled, coupled_out))

    for side in range(2):
        there = t > 0 if side == 0 else t < t_count - 1
        mine = t < t_count - 1 if side == 0 else t > 0
        columns = [
            ((s if index < 4 else partner) + 8 - 2 * (index % 4)) % 8 for index in range(8)
        ]

        @pl.when(there)
        def _():
            for index, column in enumerate(columns):
                halo_copy(side, index, column).wait_recv()

        @pl.when(mine)
        def _():
            for index, column in enumerate(columns):
                halo_copy(side, index, column).wait_send()

    row_copy(0, s, partner).wait_send()
    for turn, column in ((0, s), (1, partner)):
        for step in range(1, 4):
            row_copy(turn * 3 + step, column, partner).wait_send()
    for step in range(1, 8):
        list_copy(step).wait_send()
        far_copy(step).wait_send()

    def coef_sent(k, _):
        @pl.when(away(k))
        def _():
            coef_copy(k).wait_send()

        return 0

    lax.fori_loop(0, t_count, coef_sent, 0)
    for copy in stores:
        copy.wait()


def velocity_kernel(
    nodes,
    near_in,
    row_in,
    halo_in,
    coupled_in,
    early_in,
    worst_in,
    slots_in,
    basis_in,
    out,
    near,
    row_geometry,
    halo_geometry,
    coupled,
    early,
    early_worst,
    early_slots,
    basis,
    used,
    places,
    centre,
    features,
    spread0,
    spread1,
    moment0,
    moment1,
    kernel0,
    kernel1,
    total,
    slots,
    worst,
    columns,
    load_sem,
):
    loads = [
        pltpu.make_async_copy(source, target, load_sem.at[index])
        for index, (source, target) in enumerate(
            (
                (near_in, near),
                (row_in, row_geometry),
                (halo_in, halo_geometry),
                (worst_in, early_worst),
                (slots_in, early_slots),
                (basis_in, basis),
                (coupled_in, coupled),
                (early_in, early),
            )
        )
    ]
    for load in loads:
        load.start()
    t = lax.axis_index("tgt")
    s = lax.axis_index("src")
    own = out.shape[1]
    per_body = near.shape[1]
    total[...] = jnp.zeros_like(total)
    moment1[...] = jnp.zeros_like(moment1)
    kernel1[...] = jnp.zeros_like(kernel1)
    loads[1].wait()
    target_stage(nodes, own, lambda c: row_geometry[s * COMPS + c], centre, features)

    loads[0].wait()

    def listing(k, carry):
        n, rank, taken = carry
        i = k // per_body
        slot = k % per_body
        rank = jnp.where(slot == 0, 0, rank)
        taken = jnp.where(slot == 0, 0, taken)
        body = near[i, slot] - t * 32
        active = near[i, slot] >= 0
        inside = jnp.logical_and(body >= 0, body < 32)
        early_one = jnp.logical_and(inside, rank < EARLY)
        left = jnp.logical_and(active, jnp.logical_not(early_one))

        @pl.when(left)
        def _():
            used[n] = k
            places[n] = 7 - taken

        more = jnp.where(left, 1, 0)
        return n + more, rank + jnp.where(inside, 1, 0), taken + more

    zero = jnp.int32(0)
    n, _, _ = lax.fori_loop(0, own * per_body, listing, (zero, zero, zero))
    for k in range(2):
        used[n + k] = 0
        places[n + k] = 8

    for load in loads[2:5]:
        load.wait()
    worst[...] = early_worst[...]
    for k in range(own * COMPS):
        slots[k, 0:8] = early_slots[k]

    def rows_of(body):
        inside = jnp.logical_and(body >= 0, body < 32)
        here = jnp.where(inside, body, 0)
        there = jnp.where(inside, 0, jnp.where(body < 0, body + 32, body))
        base = (here // 4) * COMPS
        halo = (there // 4) * COMPS
        place = body % 4
        return [
            jnp.where(
                inside,
                row_geometry[base + c, pl.ds(place, 1), :],
                halo_geometry[halo + c, pl.ds(place, 1), :],
            )
            for c in range(COMPS)
        ]

    def source(m, spread, moment):
        k = used[m]
        i = k // per_body
        raw = rows_of(near[i, k % per_body] - t * 32)
        for c in range(COMPS):
            slots[i * COMPS + c, pl.ds(places[m], 1), :] = raw[c]
        live = jnp.where(m < n, F32(1.0), F32(0.0))
        source_stage(raw, i, live, centre, worst, spread, moment)

    near_pairs(
        n,
        lambda m: used[jnp.maximum(m, 0)] // per_body,
        source,
        features,
        total,
        (kernel0, moment0, spread0),
        (kernel1, moment1, spread1),
    )

    for load in loads[5:]:
        load.wait()
    row8 = lax.broadcasted_iota(jnp.int32, (8, 128), 0)
    lane8 = lax.broadcasted_iota(jnp.int32, (8, 128), 1)
    diagonal = jnp.where(lane8 // 16 == row8, coupled[...], 0.0).astype(BF16)[:, :64]
    far = []
    for c in range(3):
        flat = jnp.concatenate([basis[i, c] for i in range(own)], axis=0)
        far.append(jnp.dot(diagonal, flat, preferred_element_type=F32))

    for i in range(own):
        y = [slots[i * COMPS + c, 0:8] for c in range(3)]
        w = [slots[i * COMPS + 3 + c, 0:8] for c in range(3)]
        sums = [[], [], []]
        for node in range(MAIN, nodes):
            d = [
                row_geometry[s * COMPS + c, i : i + 1, node : node + 1] - y[c] for c in range(3)
            ]
            inverse = lax.rsqrt(d[0] * d[0] + d[1] * d[1] + d[2] * d[2])
            pull = (d[0] * w[0] + d[1] * w[1] + d[2] * w[2]) * (inverse * inverse * inverse)
            for c in range(3):
                value = w[c] * inverse + d[c] * pull
                summed = jnp.sum(value, axis=0, keepdims=True)
                sums[c].append(jnp.sum(summed, axis=1, keepdims=True))
        for c in range(3):
            tail = jnp.concatenate(sums[c], axis=1)
            out[c, i : i + 1, MAIN:nodes] = tail + far[c][i : i + 1, MAIN:nodes]

    crowded = jnp.max(worst[...]) > 0.0

    @pl.when(jnp.logical_not(crowded))
    def _():
        for i in range(own):
            at = total[i] + early[i]
            g = at[0:24] + at[24:48] + at[48:72]
            x = [
                row_geometry[s * COMPS + c, i : i + 1, :MAIN] - centre[c, i : i + 1, :MAIN]
                for c in range(3)
            ]
            plain = [g[k : k + 1] for k in range(3)]
            first = [[g[b + k : b + k + 1] for k in range(3)] for b in (8, 12, 16)]
            along = [g[b + 3 : b + 4] for b in (0, 8, 12, 16)]
            second = [g[20 + k : 21 + k] for k in range(3)]
            square = x[0] * x[0] + x[1] * x[1] + x[2] * x[2]
            inner = x[0] * plain[0] + x[1] * plain[1] + x[2] * plain[2] - along[0]
            for c in range(3):
                u = square * plain[c] + second[c] + along[1 + c] + x[c] * inner
                for k in range(3):
                    u = u - x[k] * (2.0 * first[k][c] + first[c][k])
                out[c, i : i + 1, :MAIN] = u + far[c][i : i + 1, :MAIN]

    @pl.when(crowded)
    def _():
        for i in range(own):
            for c in range(3):
                out[c, i : i + 1, :MAIN] = far[c][i : i + 1, :MAIN]

        def direct(k, _):
            i = k // per_body
            body = near[i, k % per_body]

            @pl.when(body >= 0)
            def _():
                empty = jnp.zeros((2, LANES), F32)
                rows = rows_of(body - t * 32)
                columns[...] = jnp.concatenate(rows + [empty], axis=0).T
                x = [row_geometry[s * COMPS + c, pl.ds(i, 1), :MAIN] for c in range(3)]

                def eight(q, sums):
                    block = columns[pl.ds(pl.multiple_of(q * 8, 8), 8), :]
                    d = [x[c] - block[:, c : c + 1] for c in range(3)]
                    w = [block[:, 3 + c : 4 + c] for c in range(3)]
                    inverse = lax.rsqrt(d[0] * d[0] + d[1] * d[1] + d[2] * d[2])
                    pull = d[0] * w[0] + d[1] * w[1] + d[2] * w[2]
                    pull = pull * (inverse * inverse * inverse)
                    return tuple(sums[c] + (w[c] * inverse + d[c] * pull) for c in range(3))

                start = tuple(jnp.zeros((8, MAIN), F32) for _ in range(3))
                sums = lax.fori_loop(0, ROWS // 8, eight, start)
                for c in range(3):
                    out[c, pl.ds(i, 1), :MAIN] += jnp.sum(sums[c], axis=0, keepdims=True)

            return 0

        lax.fori_loop(0, own * per_body, direct, 0)


def local(positions, weights, density, near_source, couplings, source_basis, target_basis):
    own, _, nodes = positions.shape
    vmem = pl.BlockSpec(memory_space=pltpu.VMEM)
    hbm = pl.BlockSpec(memory_space=pltpu.HBM)
    dma = pltpu.SemaphoreType.DMA
    turned = (1, 0, 2)
    centred = [
        pltpu.VMEM((4, own, LANES), F32),
        pltpu.VMEM((own, 96, MAIN), BF16),
        pltpu.VMEM((96, ROWS), BF16),
        pltpu.VMEM((96, ROWS), BF16),
        pltpu.VMEM((80, ROWS), BF16),
        pltpu.VMEM((80, ROWS), BF16),
        pltpu.VMEM((ROWS, MAIN), BF16),
        pltpu.VMEM((ROWS, MAIN), BF16),
    ]
    row_geometry, halo_geometry, coupled, early, worst, slots = pl.pallas_call(
        functools.partial(exchange_kernel, nodes),
        out_shape=(
            jax.ShapeDtypeStruct((8 * COMPS, own, LANES), F32),
            jax.ShapeDtypeStruct((16 * COMPS, own, LANES), F32),
            jax.ShapeDtypeStruct((8, 128), F32),
            jax.ShapeDtypeStruct((own, 80, MAIN), F32),
            jax.ShapeDtypeStruct((8, LANES), F32),
            jax.ShapeDtypeStruct((own * COMPS, 8, LANES), F32),
        ),
        in_specs=[hbm] * 6,
        out_specs=(hbm,) * 6,
        scratch_shapes=[
            pltpu.VMEM((8 * COMPS, own, LANES), F32),
            pltpu.VMEM((8, 128), F32),
            pltpu.VMEM((own, 80, MAIN), F32),
            pltpu.VMEM((8, LANES), F32),
            pltpu.VMEM((own * COMPS, 8, LANES), F32),
            pltpu.VMEM((3, own, nodes), F32),
            pltpu.VMEM((own, nodes), F32),
            pltpu.VMEM((3, own, nodes), F32),
            pltpu.VMEM((own, 8), jnp.int32),
            pltpu.SMEM((own, 8), jnp.int32),
            pltpu.VMEM((32, 16, 16, 128), BF16),
            pltpu.VMEM((own, 3, 16, nodes), BF16),
            pltpu.VMEM((16, 128), BF16),
            pltpu.VMEM((32, 16, 128), BF16),
            pltpu.VMEM((8, own, 128), jnp.int32),
            pltpu.VMEM((32, 128), F32),
            pltpu.VMEM((512, 128), F32),
            pltpu.VMEM((4, 8, 128), F32),
            pltpu.VMEM((7, 8, 128), F32),
            pltpu.SMEM((2 * own * EARLY,), jnp.int32),
            *centred,
            dma((7,)),
            dma((5,)),
            dma((7,)),
            dma((7,)),
            dma((32,)),
            dma((32,)),
            dma((7,)),
            dma((7,)),
            dma((7,)),
            dma((7,)),
            dma((16,)),
            dma((16,)),
        ],
        compiler_params=pltpu.CompilerParams(
            collective_id=0, has_side_effects=True, vmem_limit_bytes=VMEM_BYTES
        ),
        name="exchange",
    )(
        positions.transpose(turned),
        weights,
        density.transpose(turned),
        near_source,
        couplings.transpose(0, 2, 3, 1),
        source_basis.transpose(0, 2, 1, 3),
    )
    out = pl.pallas_call(
        functools.partial(velocity_kernel, nodes),
        out_shape=jax.ShapeDtypeStruct((3, own, nodes), F32),
        in_specs=[hbm] * 8,
        out_specs=vmem,
        scratch_shapes=[
            pltpu.SMEM((own, 8), jnp.int32),
            pltpu.VMEM((8 * COMPS, own, LANES), F32),
            pltpu.VMEM((16 * COMPS, own, LANES), F32),
            pltpu.VMEM((8, 128), F32),
            pltpu.VMEM((own, 80, MAIN), F32),
            pltpu.VMEM((8, LANES), F32),
            pltpu.VMEM((own * COMPS, 8, LANES), F32),
            pltpu.VMEM((own, 3, 16, nodes), BF16),
            pltpu.SMEM((40,), jnp.int32),
            pltpu.SMEM((40,), jnp.int32),
            *centred,
            pltpu.VMEM((own, 80, MAIN), F32),
            pltpu.VMEM((own * COMPS, 16, LANES), F32),
            pltpu.VMEM((8, LANES), F32),
            pltpu.VMEM((LANES, 8), F32),
            dma((8,)),
        ],
        compiler_params=pltpu.CompilerParams(vmem_limit_bytes=VMEM_BYTES),
        name="velocity",
    )(
        near_source,
        row_geometry,
        halo_geometry,
        coupled,
        early,
        worst,
        slots,
        target_basis.transpose(0, 2, 1, 3),
    )
    return out.transpose(turned)


def solution(mesh):
    placed = (
        P(("tgt", "src"), None, None),
        P(("tgt", "src"), None),
        P(("tgt", "src"), None, None),
        P(("tgt", "src"), None),
        P("tgt", "src", None, None),
        P(("tgt", "src"), None, None, None),
        P(("tgt", "src"), None, None, None),
    )
    return jax.shard_map(
        local, mesh=mesh, in_specs=placed, out_specs=P(("tgt", "src"), None, None), check_vma=False
    )
```

```python
import functools
import jax
import jax.numpy as jnp
from jax import lax
from jax.experimental import pallas as pl
from jax.experimental.pallas import tpu as pltpu
from jax.sharding import PartitionSpec as P

F32 = jnp.float32
BF16 = jnp.bfloat16
LANES = 768
ROWS = 656
MAIN = 640
COMPS = 6
FAR_AWAY = 1000.0
LEAST_GAP = 0.1
MOST_RATIO = 70.0
PHASES = (1, 1, 1, 2)
FACTORS = 32
MOMENTS = 48
EARLY = sum(PHASES)
CUTS = (0, 208, 432, ROWS)
VMEM_BYTES = 58 * 2**20
MESH = pl.DeviceIdType.MESH


def remote(source, target, send, recv, device):
    return pltpu.make_async_remote_copy(
        src_ref=source,
        dst_ref=target,
        send_sem=send,
        recv_sem=recv,
        device_id=device,
        device_id_type=MESH,
    )


def split(value):
    high = value.astype(BF16).astype(F32)
    rest = value - high
    middle = rest.astype(BF16).astype(F32)
    return high, middle, rest - middle


def by_quad(sub, first, second, third, fourth):
    quad = sub % 4
    return jnp.where(
        quad == 0, first, jnp.where(quad == 1, second, jnp.where(quad == 2, third, fourth))
    )


def target_stage(nodes, own, load, centre, features):
    inside = lax.broadcasted_iota(jnp.int32, (own, LANES), 1) < nodes
    radius = jnp.zeros((own, LANES), F32)
    offsets = []
    for c in range(3):
        value = load(c)
        mean = jnp.sum(jnp.where(inside, value, 0.0), axis=1, keepdims=True) / nodes
        centre[c] = jnp.broadcast_to(mean, (own, LANES))
        offset = jnp.where(inside, value - mean, 0.0)
        offsets.append(offset)
        radius = radius + offset * offset
    largest = jnp.max(radius, axis=1, keepdims=True)
    centre[3] = jnp.broadcast_to(jnp.sqrt(largest), (own, LANES))
    sub = lax.broadcasted_iota(jnp.int32, (8, LANES), 0)
    for i in range(own):
        x = [jnp.broadcast_to(offset[i : i + 1, :], (8, LANES)) for offset in offsets]
        square = jnp.broadcast_to(radius[i : i + 1, :], (8, LANES))
        high, middle, low = split(by_quad(sub, x[0], x[1], x[2], square))
        one = jnp.ones_like(square)
        stack = [
            jnp.where(sub % 4 == 3, one, jnp.where(sub < 4, high, middle)),
            jnp.where(sub < 3, low, jnp.where(sub == 3, one, high)),
            jnp.where(sub < 4, middle, jnp.where(sub == 7, low, high)),
            jnp.zeros_like(square),
        ]
        features[i] = jnp.concatenate(stack, axis=0).astype(BF16)[:, :MAIN]


def source_stage(raw, i, live, centre, worst, spread, moment):
    sub = lax.broadcasted_iota(jnp.int32, (8, LANES), 0)
    y = [jnp.broadcast_to(raw[c] - centre[c, pl.ds(i, 1), :], (8, LANES)) for c in range(3)]
    w = [jnp.broadcast_to(raw[3 + c], (8, LANES)) for c in range(3)]
    square = y[0] * y[0] + y[1] * y[1] + y[2] * y[2]
    reach = jnp.sqrt(square)
    size = jnp.broadcast_to(centre[3, pl.ds(i, 1), :], (8, LANES))
    ratio = (reach + size) - MOST_RATIO * jnp.maximum(reach - size, LEAST_GAP)
    worst[...] = jnp.maximum(worst[...], ratio)
    high, middle, low = split(by_quad(sub, -2.0 * y[0], -2.0 * y[1], -2.0 * y[2], square))
    one = jnp.ones_like(square)
    stack = [
        jnp.where(sub == 7, middle, high),
        jnp.where(sub < 3, high, jnp.where(sub == 3, low, jnp.where(sub == 7, one, middle))),
        jnp.where(sub % 4 == 3, one, jnp.where(sub < 4, middle, low)),
        jnp.zeros_like(square),
    ]
    spread[...] = jnp.concatenate(stack, axis=0).astype(BF16)[:, :ROWS]
    w = [live * value for value in w]
    along = y[0] * w[0] + y[1] * w[1] + y[2] * w[2]
    plain = by_quad(sub, w[0], w[1], w[2], one)
    last = [w[c] * square + along * y[c] for c in range(3)]
    front = plain * jnp.where(sub < 4, one, y[0])
    front = jnp.where(sub == 3, along, jnp.where(sub == 7, last[0], front))
    back = plain * jnp.where(sub < 4, y[1], y[2])
    back = jnp.where(sub == 3, last[1], jnp.where(sub == 7, last[2], back))
    fronts, backs = split(front), split(back)
    stack = [value for pair in zip(fronts, backs) for value in pair]
    moment[...] = jnp.concatenate(stack, axis=0).astype(BF16)[:, :ROWS]


def last_nodes(nodes, i, load, slots):
    y = [slots[i * COMPS + c, 0:8] for c in range(3)]
    w = [slots[i * COMPS + 3 + c, 0:8] for c in range(3)]
    sums = [[], [], []]
    for node in range(MAIN, nodes):
        d = [load(c)[i : i + 1, node : node + 1] - y[c] for c in range(3)]
        inverse = lax.rsqrt(d[0] * d[0] + d[1] * d[1] + d[2] * d[2])
        pull = (d[0] * w[0] + d[1] * w[1] + d[2] * w[2]) * (inverse * inverse * inverse)
        for c in range(3):
            summed = jnp.sum(w[c] * inverse + d[c] * pull, axis=0, keepdims=True)
            sums[c].append(jnp.sum(summed, axis=1, keepdims=True))
    return [jnp.concatenate(values, axis=1) for values in sums]


def kernel_chunk(features, spread, kernel, low, high):
    squared = lax.dot_general(
        spread[:, low:high], features, (((0,), (0,)), ((), ())), preferred_element_type=F32
    )
    inverse = lax.rsqrt(squared)
    kernel[low:high] = (inverse * inverse * inverse).astype(BF16)


def moment_chunk(kernel, moment, low, high):
    return jnp.dot(moment[:, low:high], kernel[low:high], preferred_element_type=F32)


def near_pairs(count, target_of, source, features, total, first, second):
    def turn(q, _):
        for e, (mine, other) in enumerate(((first, second), (second, first))):
            m = 2 * q + e
            for low, high in zip(CUTS[:-1], CUTS[1:]):
                kernel_chunk(features[target_of(m)], mine[2], mine[0], low, high)
                total[target_of(m - 1)] += moment_chunk(other[0], other[1], low, high)
            source(m + 1, other[2], other[1])
        return 0

    halves = (count + 1) // 2
    second[1][...] = jnp.zeros_like(second[1])
    source(0, first[2], first[1])
    lax.fori_loop(0, halves, turn, 0)
    total[target_of(2 * halves - 1)] += moment_chunk(second[0], second[1], 0, ROWS)


def exchange_kernel(
    nodes,
    positions_in,
    weights_in,
    density_in,
    near_in,
    couplings_in,
    basis_in,
    row_out,
    halo_out,
    coupled_out,
    total_out,
    worst_out,
    tails_out,
    done_out,
    own_geometry,
    partner_geometry,
    row_geometry,
    coupled,
    total,
    worst,
    tails,
    slots,
    positions,
    weights,
    density,
    near,
    near_scalar,
    held,
    basis,
    coef_mine,
    coef_parts,
    lists,
    mask,
    folded,
    far_mine,
    far_parts,
    chosen,
    done,
    centre,
    features,
    spread0,
    spread1,
    moment0,
    moment1,
    kernel0,
    kernel1,
    load_sem,
    store_sem,
    list_send,
    list_recv,
    coef_send,
    coef_recv,
    far_send,
    far_recv,
    row_send,
    row_recv,
    halo_send,
    halo_recv,
):
    t = lax.axis_index("tgt")
    s = lax.axis_index("src")
    t_count = lax.axis_size("tgt")
    quarter = t // 4
    own = positions.shape[1]
    slot_count = near.shape[1]
    loops_back = quarter == s
    partner = s + 1 - 2 * (s % 2)

    loads = [
        pltpu.make_async_copy(source, target, load_sem.at[index])
        for index, (source, target) in enumerate(
            (
                (positions_in, positions),
                (weights_in, weights),
                (density_in, density),
                (near_in, near),
                (near_in, near_scalar),
                (basis_in, basis),
                (couplings_in, held),
            )
        )
    ]
    for load in loads:
        load.start()

    barrier = pltpu.get_barrier_semaphore()

    def greet(device):
        pl.semaphore_signal(barrier, inc=1, device_id=device, device_id_type=MESH)

    for step in range(1, 8):
        greet((t, (s + step) % 8))

    def greet_source(k, _):
        @pl.when(jnp.logical_not(jnp.logical_and(loops_back, k == (t % 4) * 8 + s)))
        def _():
            greet((4 * s + k // 8, k % 8))

        return 0

    lax.fori_loop(0, t_count, greet_source, 0)

    @pl.when(t > 0)
    def _():
        greet((t - 1, s))

    @pl.when(t < t_count - 1)
    def _():
        greet((t + 1, s))

    def block(column):
        return row_geometry.at[pl.ds(column * COMPS, COMPS)]

    for load in loads[:4]:
        load.wait()
    pad = jnp.zeros((own, LANES - nodes), F32)
    for c in range(3):
        own_geometry[c] = jnp.concatenate([positions[c], pad + FAR_AWAY], axis=1)
        own_geometry[3 + c] = jnp.concatenate([density[c] * weights[...], pad], axis=1)
    lists[s] = jnp.concatenate([near[...], jnp.full((own, 120), -1, jnp.int32)], axis=1)

    loads[5].wait()
    sub16 = lax.broadcasted_iota(jnp.int32, (16, 128), 0)
    lane16 = lax.broadcasted_iota(jnp.int32, (16, 128), 1)
    spread = jnp.zeros((16, 128), F32)
    for j in range(own):
        product = basis[j, 0].astype(F32) * density[0, j : j + 1, :]
        for c in range(1, 3):
            product = product + basis[j, c].astype(F32) * density[c, j : j + 1, :]
        value = jnp.sum(product, axis=1, keepdims=True)
        spread = jnp.where(lane16 == sub16 + 16 * j, value, spread)
    coef_mine[...] = jnp.sum(spread, axis=0, keepdims=True).astype(BF16).astype(F32)

    pl.semaphore_wait(
        barrier,
        7
        + t_count
        - jnp.where(loops_back, 1, 0)
        + jnp.where(t > 0, 1, 0)
        + jnp.where(t < t_count - 1, 1, 0),
    )

    def partner_copy():
        return remote(
            own_geometry, partner_geometry, row_send.at[0], row_recv.at[0], (t, partner)
        )

    def row_copy(turn, step, source, column, device):
        return remote(
            source,
            block(column),
            row_send.at[turn * 3 + step],
            row_recv.at[turn * 3 + step],
            (t, device),
        )

    def halo_copy(side, index, source, column):
        return remote(
            source,
            halo_out.at[pl.ds((side * 8 + column) * COMPS, COMPS)],
            halo_send.at[side * 8 + index],
            halo_recv.at[side * 8 + index],
            (t + 1 - 2 * side, s),
        )

    def halo_start(index, source, column):
        @pl.when(t < t_count - 1)
        def _():
            halo_copy(0, index, source, column).start()

        @pl.when(t > 0)
        def _():
            halo_copy(1, index, source, column).start()

    def across_start(turn, source, column):
        for step in range(1, 4):
            row_copy(turn, step, source, column, (s + 2 * step) % 8).start()
        halo_start(4 * turn, source, column)

    def across_wait(turn, source, column):
        for step in range(1, 4):
            here = (column + 8 - 2 * step) % 8
            row_copy(turn, step, source, here, partner).wait_recv()
            halo_start(4 * turn + step, block(here), here)

    def coef_copy(k):
        return remote(
            coef_mine,
            coef_parts.at[(t % 4) * 8 + s],
            coef_send.at[k],
            coef_recv.at[(t % 4) * 8 + s],
            (k, quarter),
        )

    def away(k):
        return jnp.logical_not(jnp.logical_and(loops_back, k == t))

    def coef_start(k, _):
        @pl.when(away(k))
        def _():
            coef_copy(k).start()

        return 0

    def list_copy(step):
        return remote(
            lists.at[s],
            lists.at[s],
            list_send.at[step - 1],
            list_recv.at[step - 1],
            (t, (s + step) % 8),
        )

    partner_copy().start()
    for step in range(1, 8):
        list_copy(step).start()
    lax.fori_loop(0, t_count, coef_start, 0)
    across_start(0, own_geometry, s)

    @pl.when(loops_back)
    def _():
        coef_parts[(t % 4) * 8 + s] = coef_mine[...]

    loads[4].wait()

    def choose(i, _):
        bodies = [near_scalar[i, k] - t * 32 for k in range(slot_count)]
        free = [jnp.where(body >= 0, 1, 0) * jnp.where(body < 32, 1, 0) for body in bodies]
        taken = [jnp.int32(0)] * slot_count
        first = 0
        for phase, count in enumerate(PHASES):
            device = (s, partner, partner, None)[phase]
            other = s * 4 + (i + 1) % own if phase in (0, 3) else partner * 4
            for e in range(count):
                pick = jnp.int32(0) + other
                live = jnp.int32(0)
                for k in range(slot_count):
                    hit = free[k] * (1 - live)
                    if device is not None:
                        hit = hit * jnp.where(bodies[k] // 4 == device, 1, 0)
                    pick = jnp.where(hit == 1, bodies[k], pick)
                    live = live + hit
                    free[k] = free[k] - hit
                    taken[k] = taken[k] + hit
                place = first * own + i * count + e
                chosen[2 * place] = pick
                chosen[2 * place + 1] = live
            first = first + count
        for k in range(slot_count):
            done[i, k] = taken[k]
        return 0

    lax.fori_loop(0, own, choose, 0)

    target_stage(nodes, own, lambda c: own_geometry[c], centre, features)
    total[...] = jnp.zeros_like(total)
    worst[...] = jnp.full_like(worst, -1.0)
    for k in range(own * COMPS):
        slots[k] = jnp.full((8, LANES), FAR_AWAY if k % COMPS < 3 else 0.0, F32)
    kernel1[...] = jnp.zeros_like(kernel1)

    first_set = (kernel0, moment0, spread0)
    second_set = (kernel1, moment1, spread1)

    def early_pairs(phase, geometry, device):
        count = PHASES[phase]
        first = sum(PHASES[:phase])
        last = own * count - 1

        def source(m, spread, moment):
            now = jnp.minimum(m, last)
            i = now // count
            e = now % count
            place = first * own + now
            body = chosen[2 * place]
            live = chosen[2 * place + 1].astype(F32)
            base = 0 if device is not None else (body // 4) * COMPS
            raw = [geometry[base + c, pl.ds(body % 4, 1), :] for c in range(COMPS)]
            for c in range(3):
                slots[i * COMPS + c, pl.ds(first + e, 1), :] = raw[c]
                slots[i * COMPS + 3 + c, pl.ds(first + e, 1), :] = raw[3 + c] * live
            scale = live * jnp.where(m <= last, F32(1.0), F32(0.0))
            source_stage(raw, i, scale, centre, worst, spread, moment)

        def target_of(m):
            return jnp.clip(m, 0, last) // count

        near_pairs(last + 1, target_of, source, features, total, first_set, second_set)

    early_pairs(0, own_geometry, s)

    across_wait(0, own_geometry, s)
    partner_copy().wait_recv()
    across_start(1, partner_geometry, partner)
    for c in range(COMPS):
        row_geometry[s * COMPS + c] = own_geometry[c]
        row_geometry[partner * COMPS + c] = partner_geometry[c]

    early_pairs(1, partner_geometry, partner)

    for step in range(1, 8):
        remote(
            lists.at[s],
            lists.at[(s + 8 - step) % 8],
            list_send.at[step - 1],
            list_recv.at[step - 1],
            (t, partner),
        ).wait_recv()
    rows = 8 * own
    listed = lists[...].reshape(rows, 128)
    ids = s * 128 + lax.broadcasted_iota(jnp.int32, (rows, 128), 1)
    hit = ids == t * rows + lax.broadcasted_iota(jnp.int32, (rows, 128), 0)
    for k in range(slot_count):
        hit = jnp.logical_or(hit, ids == listed[:, k : k + 1])
    mask[...] = jnp.where(hit, F32(0.0), F32(1.0))

    def coef_wait(k, _):
        @pl.when(jnp.logical_not(jnp.logical_and(loops_back, k == (t % 4) * 8 + s)))
        def _():
            remote(
                coef_mine, coef_parts.at[k], coef_send.at[k], coef_recv.at[k], (t, partner)
            ).wait_recv()

        return 0

    lax.fori_loop(0, t_count, coef_wait, 0)
    gathered = coef_parts[...].reshape(t_count, 128).astype(BF16)
    from_row = lax.broadcasted_iota(jnp.int32, (t_count, 128), 0)
    to_lane = lax.broadcasted_iota(jnp.int32, (t_count, 128), 1)
    coef = jnp.zeros((16, 128), F32)
    for j in range(own):
        chooser = jnp.where(to_lane == own * from_row + j, F32(1.0), F32(0.0)).astype(BF16)
        coef = coef + lax.dot_general(
            gathered[:, 16 * j : 16 * j + 16],
            chooser,
            (((0,), (0,)), ((), ())),
            preferred_element_type=F32,
        )
    loads[6].wait()

    def fold(i, _):
        kept = coef * mask[pl.ds(i, 1), :]
        product = held[i].astype(F32) * kept[None]
        folded[pl.ds(pl.multiple_of(i * 16, 16), 16), :] = jnp.sum(product, axis=1)
        return 0

    lax.fori_loop(0, rows, fold, 0)
    for q in range(4):
        turned = folded[q * 128 : (q + 1) * 128, :].T
        far_mine[q] = jnp.sum(turned, axis=0, keepdims=True)

    def far_copy(step):
        other = (s + step) % 8
        return remote(
            far_mine.at[other // 2],
            far_parts.at[step - 1],
            far_send.at[step - 1],
            far_recv.at[step - 1],
            (t, other),
        )

    for step in range(1, 8):
        far_copy(step).start()

    early_pairs(2, partner_geometry, partner)
    across_wait(1, partner_geometry, partner)

    def store(index, source, target):
        copy = pltpu.make_async_copy(source, target, store_sem.at[index])
        copy.start()
        return copy

    stores = [store(0, row_geometry, row_out), store(5, done, done_out)]
    early_pairs(3, row_geometry, None)
    stores.append(store(1, total, total_out))
    stores.append(store(2, worst, worst_out))
    for i in range(own):
        sums = last_nodes(nodes, i, lambda c: own_geometry[c], slots)
        for c in range(3):
            empty = jnp.zeros((1, 128 + MAIN - nodes), F32)
            tails[c, i : i + 1, :] = jnp.concatenate([sums[c], empty], axis=1)
    stores.append(store(3, tails, tails_out))

    for step in range(1, 8):
        far_copy(step).wait_recv()
    w = far_mine[s // 2]
    for step in range(1, 8):
        w = w + far_parts[step - 1]
    w = jnp.broadcast_to(w, (8, 128))
    coupled[...] = jnp.where(s % 2 == 1, pltpu.roll(w, 64, 1), w)

    stores.append(store(4, coupled, coupled_out))

    for side in range(2):
        there = t > 0 if side == 0 else t < t_count - 1
        mine = t < t_count - 1 if side == 0 else t > 0
        columns = [
            ((s if index < 4 else partner) + 8 - 2 * (index % 4)) % 8 for index in range(8)
        ]

        @pl.when(there)
        def _():
            for index, column in enumerate(columns):
                halo_copy(side, index, own_geometry, column).wait_recv()

        @pl.when(mine)
        def _():
            for index, column in enumerate(columns):
                halo_copy(side, index, own_geometry, column).wait_send()

    partner_copy().wait_send()
    for turn, column in ((0, s), (1, partner)):
        for step in range(1, 4):
            row_copy(turn, step, own_geometry, column, partner).wait_send()
    for step in range(1, 8):
        list_copy(step).wait_send()
        far_copy(step).wait_send()

    def coef_sent(k, _):
        @pl.when(away(k))
        def _():
            coef_copy(k).wait_send()

        return 0

    lax.fori_loop(0, t_count, coef_sent, 0)
    for copy in stores:
        copy.wait()


def velocity_kernel(
    nodes,
    near_in,
    row_in,
    halo_in,
    coupled_in,
    early_in,
    worst_in,
    tails_in,
    done_in,
    basis_in,
    out,
    near,
    done,
    row_geometry,
    halo_geometry,
    coupled,
    early,
    early_worst,
    early_tail,
    basis,
    used,
    places,
    centre,
    features,
    spread0,
    spread1,
    moment0,
    moment1,
    kernel0,
    kernel1,
    total,
    slots,
    worst,
    columns,
    load_sem,
):
    loads = [
        pltpu.make_async_copy(source, target, load_sem.at[index])
        for index, (source, target) in enumerate(
            (
                (near_in, near),
                (done_in, done),
                (row_in, row_geometry),
                (halo_in, halo_geometry),
                (worst_in, early_worst),
                (tails_in, early_tail),
                (basis_in, basis),
                (coupled_in, coupled),
                (early_in, early),
            )
        )
    ]
    for load in loads:
        load.start()
    t = lax.axis_index("tgt")
    s = lax.axis_index("src")
    own = out.shape[1]
    per_body = near.shape[1]
    total[...] = jnp.zeros_like(total)
    kernel1[...] = jnp.zeros_like(kernel1)
    loads[2].wait()
    target_stage(nodes, own, lambda c: row_geometry[s * COMPS + c], centre, features)

    for load in loads[:2]:
        load.wait()

    def listing(k, carry):
        n, taken = carry
        i = k // per_body
        slot = k % per_body
        taken = jnp.where(slot == 0, 0, taken)
        left = jnp.logical_and(near[i, slot] >= 0, done[i, slot] == 0)

        @pl.when(left)
        def _():
            used[n] = k
            places[n] = taken

        more = jnp.where(left, 1, 0)
        return n + more, taken + more

    n, _ = lax.fori_loop(0, own * per_body, listing, (jnp.int32(0), jnp.int32(0)))
    for k in range(2):
        used[n + k] = 0
        places[n + k] = 8

    for load in loads[3:6]:
        load.wait()
    worst[...] = early_worst[...]
    for k in range(own * COMPS):
        slots[k, 0:8] = jnp.full((8, LANES), FAR_AWAY if k % COMPS < 3 else 0.0, F32)

    def rows_of(body):
        inside = jnp.logical_and(body >= 0, body < 32)
        here = jnp.where(inside, body, 0)
        there = jnp.where(inside, 0, jnp.where(body < 0, body + 32, body))
        base = (here // 4) * COMPS
        halo = (there // 4) * COMPS
        place = body % 4
        return [
            jnp.where(
                inside,
                row_geometry[base + c, pl.ds(place, 1), :],
                halo_geometry[halo + c, pl.ds(place, 1), :],
            )
            for c in range(COMPS)
        ]

    def source(m, spread, moment):
        k = used[m]
        i = k // per_body
        raw = rows_of(near[i, k % per_body] - t * 32)
        live = jnp.where(m < n, F32(1.0), F32(0.0))
        for c in range(3):
            slots[i * COMPS + c, pl.ds(places[m], 1), :] = raw[c]
            slots[i * COMPS + 3 + c, pl.ds(places[m], 1), :] = raw[3 + c] * live
        source_stage(raw, i, live, centre, worst, spread, moment)

    near_pairs(
        n,
        lambda m: used[jnp.maximum(m, 0)] // per_body,
        source,
        features,
        total,
        (kernel0, moment0, spread0),
        (kernel1, moment1, spread1),
    )

    for load in loads[6:]:
        load.wait()
    row8 = lax.broadcasted_iota(jnp.int32, (8, 128), 0)
    lane8 = lax.broadcasted_iota(jnp.int32, (8, 128), 1)
    diagonal = jnp.where(lane8 // 16 == row8, coupled[...], 0.0).astype(BF16)[:, :64]
    far = []
    for c in range(3):
        flat = jnp.concatenate([basis[i, c] for i in range(own)], axis=0)
        far.append(jnp.dot(diagonal, flat, preferred_element_type=F32))

    for i in range(own):
        sums = last_nodes(nodes, i, lambda c: row_geometry[s * COMPS + c], slots)
        for c in range(3):
            tail = sums[c] + early_tail[c, i : i + 1, 0 : nodes - MAIN]
            out[c, i : i + 1, MAIN:nodes] = tail + far[c][i : i + 1, MAIN:nodes]

    crowded = jnp.max(worst[...]) > 0.0

    @pl.when(jnp.logical_not(crowded))
    def _():
        for i in range(own):
            at = total[i] + early[i]
            g = at[0:16] + at[16:32] + at[32:48]
            x = [
                row_geometry[s * COMPS + c, i : i + 1, :MAIN] - centre[c, i : i + 1, :MAIN]
                for c in range(3)
            ]
            plain = [g[k : k + 1] for k in range(3)]
            first = [[g[b + k : b + k + 1] for k in range(3)] for b in (4, 8, 12)]
            last = [g[k : k + 1] for k in (7, 11, 15)]
            square = x[0] * x[0] + x[1] * x[1] + x[2] * x[2]
            inner = x[0] * plain[0] + x[1] * plain[1] + x[2] * plain[2] - g[3:4]
            for c in range(3):
                u = square * plain[c] + last[c] + x[c] * inner
                for k in range(3):
                    u = u - x[k] * (2.0 * first[k][c] + first[c][k])
                out[c, i : i + 1, :MAIN] = u + far[c][i : i + 1, :MAIN]

    @pl.when(crowded)
    def _():
        for i in range(own):
            for c in range(3):
                out[c, i : i + 1, :MAIN] = far[c][i : i + 1, :MAIN]

        def direct(k, _):
            i = k // per_body
            body = near[i, k % per_body]

            @pl.when(body >= 0)
            def _():
                empty = jnp.zeros((2, LANES), F32)
                rows = rows_of(body - t * 32)
                columns[...] = jnp.concatenate(rows + [empty], axis=0).T
                x = [row_geometry[s * COMPS + c, pl.ds(i, 1), :MAIN] for c in range(3)]

                def eight(q, sums):
                    block = columns[pl.ds(pl.multiple_of(q * 8, 8), 8), :]
                    d = [x[c] - block[:, c : c + 1] for c in range(3)]
                    w = [block[:, 3 + c : 4 + c] for c in range(3)]
                    inverse = lax.rsqrt(d[0] * d[0] + d[1] * d[1] + d[2] * d[2])
                    pull = d[0] * w[0] + d[1] * w[1] + d[2] * w[2]
                    pull = pull * (inverse * inverse * inverse)
                    return tuple(sums[c] + (w[c] * inverse + d[c] * pull) for c in range(3))

                start = tuple(jnp.zeros((8, MAIN), F32) for _ in range(3))
                sums = lax.fori_loop(0, ROWS // 8, eight, start)
                for c in range(3):
                    out[c, pl.ds(i, 1), :MAIN] += jnp.sum(sums[c], axis=0, keepdims=True)

            return 0

        lax.fori_loop(0, own * per_body, direct, 0)


def local(positions, weights, density, near_source, couplings, source_basis, target_basis):
    own, _, nodes = positions.shape
    vmem = pl.BlockSpec(memory_space=pltpu.VMEM)
    hbm = pl.BlockSpec(memory_space=pltpu.HBM)
    dma = pltpu.SemaphoreType.DMA
    turned = (1, 0, 2)
    centred = [
        pltpu.VMEM((4, own, LANES), F32),
        pltpu.VMEM((own, FACTORS, MAIN), BF16),
        pltpu.VMEM((FACTORS, ROWS), BF16),
        pltpu.VMEM((FACTORS, ROWS), BF16),
        pltpu.VMEM((MOMENTS, ROWS), BF16),
        pltpu.VMEM((MOMENTS, ROWS), BF16),
        pltpu.VMEM((ROWS, MAIN), BF16),
        pltpu.VMEM((ROWS, MAIN), BF16),
    ]
    moved = pl.pallas_call(
        functools.partial(exchange_kernel, nodes),
        out_shape=(
            jax.ShapeDtypeStruct((8 * COMPS, own, LANES), F32),
            jax.ShapeDtypeStruct((16 * COMPS, own, LANES), F32),
            jax.ShapeDtypeStruct((8, 128), F32),
            jax.ShapeDtypeStruct((own, MOMENTS, MAIN), F32),
            jax.ShapeDtypeStruct((8, LANES), F32),
            jax.ShapeDtypeStruct((3, own, 128), F32),
            jax.ShapeDtypeStruct((own, 8), jnp.int32),
        ),
        in_specs=[hbm] * 6,
        out_specs=(hbm,) * 7,
        scratch_shapes=[
            pltpu.VMEM((COMPS, own, LANES), F32),
            pltpu.VMEM((COMPS, own, LANES), F32),
            pltpu.VMEM((8 * COMPS, own, LANES), F32),
            pltpu.VMEM((8, 128), F32),
            pltpu.VMEM((own, MOMENTS, MAIN), F32),
            pltpu.VMEM((8, LANES), F32),
            pltpu.VMEM((3, own, 128), F32),
            pltpu.VMEM((own * COMPS, 8, LANES), F32),
            pltpu.VMEM((3, own, nodes), F32),
            pltpu.VMEM((own, nodes), F32),
            pltpu.VMEM((3, own, nodes), F32),
            pltpu.VMEM((own, 8), jnp.int32),
            pltpu.SMEM((own, 8), jnp.int32),
            pltpu.VMEM((32, 16, 16, 128), BF16),
            pltpu.VMEM((own, 3, 16, nodes), BF16),
            pltpu.VMEM((1, 128), F32),
            pltpu.VMEM((32, 1, 128), F32),
            pltpu.VMEM((8, own, 128), jnp.int32),
            pltpu.VMEM((32, 128), F32),
            pltpu.VMEM((512, 128), F32),
            pltpu.VMEM((4, 1, 128), F32),
            pltpu.VMEM((7, 1, 128), F32),
            pltpu.SMEM((2 * own * EARLY,), jnp.int32),
            pltpu.SMEM((own, 8), jnp.int32),
            *centred,
            dma((7,)),
            dma((6,)),
            dma((7,)),
            dma((7,)),
            dma((32,)),
            dma((32,)),
            dma((7,)),
            dma((7,)),
            dma((7,)),
            dma((7,)),
            dma((16,)),
            dma((16,)),
        ],
        compiler_params=pltpu.CompilerParams(
            collective_id=0, has_side_effects=True, vmem_limit_bytes=VMEM_BYTES
        ),
        name="exchange",
    )(
        positions.transpose(turned),
        weights,
        density.transpose(turned),
        near_source,
        couplings.transpose(0, 2, 3, 1),
        source_basis.transpose(0, 2, 1, 3),
    )
    out = pl.pallas_call(
        functools.partial(velocity_kernel, nodes),
        out_shape=jax.ShapeDtypeStruct((3, own, nodes), F32),
        in_specs=[hbm] * 9,
        out_specs=vmem,
        scratch_shapes=[
            pltpu.SMEM((own, 8), jnp.int32),
            pltpu.SMEM((own, 8), jnp.int32),
            pltpu.VMEM((8 * COMPS, own, LANES), F32),
            pltpu.VMEM((16 * COMPS, own, LANES), F32),
            pltpu.VMEM((8, 128), F32),
            pltpu.VMEM((own, MOMENTS, MAIN), F32),
            pltpu.VMEM((8, LANES), F32),
            pltpu.VMEM((3, own, 128), F32),
            pltpu.VMEM((own, 3, 16, nodes), BF16),
            pltpu.SMEM((40,), jnp.int32),
            pltpu.SMEM((40,), jnp.int32),
            *centred,
            pltpu.VMEM((own, MOMENTS, MAIN), F32),
            pltpu.VMEM((own * COMPS, 16, LANES), F32),
            pltpu.VMEM((8, LANES), F32),
            pltpu.VMEM((LANES, 8), F32),
            dma((9,)),
        ],
        compiler_params=pltpu.CompilerParams(vmem_limit_bytes=VMEM_BYTES),
        name="velocity",
    )(
        near_source,
        *moved,
        target_basis.transpose(0, 2, 1, 3),
    )
    return out.transpose(turned)


def solution(mesh):
    placed = (
        P(("tgt", "src"), None, None),
        P(("tgt", "src"), None),
        P(("tgt", "src"), None, None),
        P(("tgt", "src"), None),
        P("tgt", "src", None, None),
        P(("tgt", "src"), None, None, None),
        P(("tgt", "src"), None, None, None),
    )
    return jax.shard_map(
        local, mesh=mesh, in_specs=placed, out_specs=P(("tgt", "src"), None, None), check_vma=False
    )
```

```python
import functools
import jax
import jax.numpy as jnp
from jax import lax
from jax.experimental import pallas as pl
from jax.experimental.pallas import tpu as pltpu
from jax.sharding import PartitionSpec as P

F32 = jnp.float32
BF16 = jnp.bfloat16
LANES = 768
ROWS = 656
MAIN = 640
COMPS = 6
FAR_AWAY = 1000.0
LEAST_GAP = 0.1
MOST_RATIO = 70.0
PHASES = (2, 1, 1, 1)
FACTORS = 32
MOMENTS = 48
EARLY = sum(PHASES)
CUTS = (0, 256, 512, ROWS)
VMEM_BYTES = 56 * 2**20
MESH = pl.DeviceIdType.MESH


def remote(source, target, send, recv, device):
    return pltpu.make_async_remote_copy(
        src_ref=source,
        dst_ref=target,
        send_sem=send,
        recv_sem=recv,
        device_id=device,
        device_id_type=MESH,
    )


def split(value):
    high = value.astype(BF16).astype(F32)
    rest = value - high
    middle = rest.astype(BF16).astype(F32)
    return high, middle, rest - middle


def by_quad(sub, first, second, third, fourth):
    quad = sub % 4
    return jnp.where(
        quad == 0, first, jnp.where(quad == 1, second, jnp.where(quad == 2, third, fourth))
    )


def target_stage(nodes, own, load, centre, features):
    inside = lax.broadcasted_iota(jnp.int32, (own, LANES), 1) < nodes
    radius = jnp.zeros((own, LANES), F32)
    offsets = []
    for c in range(3):
        value = load(c)
        mean = jnp.sum(jnp.where(inside, value, 0.0), axis=1, keepdims=True) / nodes
        centre[c] = jnp.broadcast_to(mean, (own, LANES))
        offset = jnp.where(inside, value - mean, 0.0)
        offsets.append(offset)
        radius = radius + offset * offset
    largest = jnp.max(radius, axis=1, keepdims=True)
    centre[3] = jnp.broadcast_to(jnp.sqrt(largest), (own, LANES))
    sub = lax.broadcasted_iota(jnp.int32, (8, LANES), 0)
    for i in range(own):
        x = [jnp.broadcast_to(offset[i : i + 1, :], (8, LANES)) for offset in offsets]
        square = jnp.broadcast_to(radius[i : i + 1, :], (8, LANES))
        high, middle, low = split(by_quad(sub, x[0], x[1], x[2], square))
        one = jnp.ones_like(square)
        stack = [
            jnp.where(sub % 4 == 3, one, jnp.where(sub < 4, high, middle)),
            jnp.where(sub < 3, low, jnp.where(sub == 3, one, high)),
            jnp.where(sub < 4, middle, jnp.where(sub == 7, low, high)),
            jnp.zeros_like(square),
        ]
        features[i] = jnp.concatenate(stack, axis=0).astype(BF16)[:, :MAIN]


def source_stage(raw, i, live, centre, worst, spread, moment):
    sub = lax.broadcasted_iota(jnp.int32, (8, LANES), 0)
    y = [jnp.broadcast_to(raw[c] - centre[c, pl.ds(i, 1), :], (8, LANES)) for c in range(3)]
    w = [jnp.broadcast_to(raw[3 + c], (8, LANES)) for c in range(3)]
    square = y[0] * y[0] + y[1] * y[1] + y[2] * y[2]
    reach = jnp.sqrt(square)
    size = jnp.broadcast_to(centre[3, pl.ds(i, 1), :], (8, LANES))
    ratio = (reach + size) - MOST_RATIO * jnp.maximum(reach - size, LEAST_GAP)
    worst[...] = jnp.maximum(worst[...], ratio)
    high, middle, low = split(by_quad(sub, -2.0 * y[0], -2.0 * y[1], -2.0 * y[2], square))
    one = jnp.ones_like(square)
    stack = [
        jnp.where(sub == 7, middle, high),
        jnp.where(sub < 3, high, jnp.where(sub == 3, low, jnp.where(sub == 7, one, middle))),
        jnp.where(sub % 4 == 3, one, jnp.where(sub < 4, middle, low)),
        jnp.zeros_like(square),
    ]
    spread[...] = jnp.concatenate(stack, axis=0).astype(BF16)[:, :ROWS]
    w = [live * value for value in w]
    along = y[0] * w[0] + y[1] * w[1] + y[2] * w[2]
    plain = by_quad(sub, w[0], w[1], w[2], one)
    last = [w[c] * square + along * y[c] for c in range(3)]
    front = plain * jnp.where(sub < 4, one, y[0])
    front = jnp.where(sub == 3, along, jnp.where(sub == 7, last[0], front))
    back = plain * jnp.where(sub < 4, y[1], y[2])
    back = jnp.where(sub == 3, last[1], jnp.where(sub == 7, last[2], back))
    fronts, backs = split(front), split(back)
    stack = [value for pair in zip(fronts, backs) for value in pair]
    moment[...] = jnp.concatenate(stack, axis=0).astype(BF16)[:, :ROWS]


def last_nodes(nodes, i, load, slots):
    y = [slots[i * COMPS + c, 0:8] for c in range(3)]
    w = [slots[i * COMPS + 3 + c, 0:8] for c in range(3)]
    sums = [[], [], []]
    for node in range(MAIN, nodes):
        d = [load(c)[i : i + 1, node : node + 1] - y[c] for c in range(3)]
        inverse = lax.rsqrt(d[0] * d[0] + d[1] * d[1] + d[2] * d[2])
        pull = (d[0] * w[0] + d[1] * w[1] + d[2] * w[2]) * (inverse * inverse * inverse)
        for c in range(3):
            summed = jnp.sum(w[c] * inverse + d[c] * pull, axis=0, keepdims=True)
            sums[c].append(jnp.sum(summed, axis=1, keepdims=True))
    return [jnp.concatenate(values, axis=1) for values in sums]


def kernel_chunk(features, spread, kernel, low, high):
    squared = lax.dot_general(
        spread[:, low:high], features, (((0,), (0,)), ((), ())), preferred_element_type=F32
    )
    inverse = lax.rsqrt(squared)
    kernel[low:high] = (inverse * inverse * inverse).astype(BF16)


def moment_chunk(kernel, moment, low, high):
    return jnp.dot(moment[:, low:high], kernel[low:high], preferred_element_type=F32)


def near_pairs(count, target_of, source, features, total, first, second):
    def turn(q, _):
        for e, (mine, other) in enumerate(((first, second), (second, first))):
            m = 2 * q + e
            for low, high in zip(CUTS[:-1], CUTS[1:]):
                kernel_chunk(features[target_of(m)], mine[2], mine[0], low, high)
                total[target_of(m - 1)] += moment_chunk(other[0], other[1], low, high)
            source(m + 1, other[2], other[1])
        return 0

    halves = (count + 1) // 2
    second[1][...] = jnp.zeros_like(second[1])
    source(0, first[2], first[1])
    lax.fori_loop(0, halves, turn, 0)
    total[target_of(2 * halves - 1)] += moment_chunk(second[0], second[1], 0, ROWS)


def exchange_kernel(
    nodes,
    positions_in,
    weights_in,
    density_in,
    near_in,
    couplings_in,
    basis_in,
    row_geometry,
    halo_geometry,
    coupled,
    total,
    worst,
    tails,
    done_out,
    own_geometry,
    partner_geometry,
    slots,
    positions,
    weights,
    density,
    near,
    near_scalar,
    held,
    basis,
    coef_mine,
    coef_parts,
    lists,
    mask,
    folded,
    far_mine,
    far_parts,
    chosen,
    done,
    centre,
    features,
    spread0,
    spread1,
    moment0,
    moment1,
    kernel0,
    kernel1,
    load_sem,
    store_sem,
    list_send,
    list_recv,
    coef_send,
    coef_recv,
    far_send,
    far_recv,
    row_send,
    row_recv,
    halo_send,
    halo_recv,
):
    t = lax.axis_index("tgt")
    s = lax.axis_index("src")
    t_count = lax.axis_size("tgt")
    quarter = t // 4
    own = positions.shape[1]
    slot_count = near.shape[1]
    loops_back = quarter == s
    partner = s + 1 - 2 * (s % 2)

    loads = [
        pltpu.make_async_copy(source, target, load_sem.at[index])
        for index, (source, target) in enumerate(
            (
                (positions_in, positions),
                (weights_in, weights),
                (density_in, density),
                (near_in, near),
                (near_in, near_scalar),
                (basis_in, basis),
                (couplings_in, held),
            )
        )
    ]
    for load in loads:
        load.start()

    barrier = pltpu.get_barrier_semaphore()

    def greet(device):
        pl.semaphore_signal(barrier, inc=1, device_id=device, device_id_type=MESH)

    for step in range(1, 8):
        greet((t, (s + step) % 8))

    def every(act, mine):
        for k in range(t_count - 1):
            act(k + jnp.where(jnp.logical_and(loops_back, mine <= k), 1, 0))

        @pl.when(jnp.logical_not(loops_back))
        def _():
            act(t_count - 1)

    as_source = (t % 4) * 8 + s

    @pl.when(t > 0)
    def _():
        greet((t - 1, s))

    @pl.when(t < t_count - 1)
    def _():
        greet((t + 1, s))

    every(lambda k: greet((4 * s + k // 8, k % 8)), as_source)

    def block(column):
        return row_geometry.at[pl.ds(column * COMPS, COMPS)]

    for load in loads[:4]:
        load.wait()
    pad = jnp.zeros((own, LANES - nodes), F32)
    for c in range(3):
        own_geometry[c] = jnp.concatenate([positions[c], pad + FAR_AWAY], axis=1)
        own_geometry[3 + c] = jnp.concatenate([density[c] * weights[...], pad], axis=1)
    lists[s] = jnp.concatenate([near[...], jnp.full((own, 120), -1, jnp.int32)], axis=1)

    loads[5].wait()
    sub16 = lax.broadcasted_iota(jnp.int32, (16, 128), 0)
    lane16 = lax.broadcasted_iota(jnp.int32, (16, 128), 1)
    spread = jnp.zeros((16, 128), F32)
    for j in range(own):
        product = basis[j, 0].astype(F32) * density[0, j : j + 1, :]
        for c in range(1, 3):
            product = product + basis[j, c].astype(F32) * density[c, j : j + 1, :]
        value = jnp.sum(product, axis=1, keepdims=True)
        spread = jnp.where(lane16 == sub16 + 16 * j, value, spread)
    coef_mine[...] = jnp.sum(spread, axis=0, keepdims=True).astype(BF16).astype(F32)

    pl.semaphore_wait(
        barrier,
        7
        + t_count
        - jnp.where(loops_back, 1, 0)
        + jnp.where(t > 0, 1, 0)
        + jnp.where(t < t_count - 1, 1, 0),
    )

    def partner_copy():
        return remote(
            own_geometry, partner_geometry, row_send.at[0], row_recv.at[0], (t, partner)
        )

    def row_copy(turn, step, source, column, device):
        return remote(
            source,
            block(column),
            row_send.at[turn * 3 + step],
            row_recv.at[turn * 3 + step],
            (t, device),
        )

    def halo_copy(side, index, source, column):
        return remote(
            source,
            halo_geometry.at[pl.ds((side * 8 + column) * COMPS, COMPS)],
            halo_send.at[side * 8 + index],
            halo_recv.at[side * 8 + index],
            (t + 1 - 2 * side, s),
        )

    def halo_start(index, source, column):
        @pl.when(t < t_count - 1)
        def _():
            halo_copy(0, index, source, column).start()

        @pl.when(t > 0)
        def _():
            halo_copy(1, index, source, column).start()

    def across_start(turn, source, column):
        for step in range(1, 4):
            row_copy(turn, step, source, column, (s + 2 * step) % 8).start()
        halo_start(4 * turn, source, column)

    def across_wait(turn, source, column):
        for step in range(1, 4):
            here = (column + 8 - 2 * step) % 8
            row_copy(turn, step, source, here, partner).wait_recv()
            halo_start(4 * turn + step, block(here), here)

    def coef_copy(k):
        return remote(
            coef_mine,
            coef_parts.at[(t % 4) * 8 + s],
            coef_send.at[k],
            coef_recv.at[(t % 4) * 8 + s],
            (k, quarter),
        )

    def list_copy(step):
        return remote(
            lists.at[s],
            lists.at[s],
            list_send.at[step - 1],
            list_recv.at[step - 1],
            (t, (s + step) % 8),
        )

    partner_copy().start()
    for step in range(1, 8):
        list_copy(step).start()
    every(lambda k: coef_copy(k).start(), t)
    across_start(0, own_geometry, s)

    @pl.when(loops_back)
    def _():
        coef_parts[(t % 4) * 8 + s] = coef_mine[...]

    loads[4].wait()

    def choose(i, _):
        bodies = [near_scalar[i, k] - t * 32 for k in range(slot_count)]
        free = [jnp.where(body >= 0, 1, 0) * jnp.where(body < 32, 1, 0) for body in bodies]
        taken = [jnp.int32(0)] * slot_count
        first = 0
        for phase, count in enumerate(PHASES):
            device = (s, partner, partner, None)[phase]
            other = s * 4 + (i + 1) % own if phase in (0, 3) else partner * 4
            for e in range(count):
                pick = jnp.int32(0) + other
                live = jnp.int32(0)
                for k in range(slot_count):
                    hit = free[k] * (1 - live)
                    if device is not None:
                        hit = hit * jnp.where(bodies[k] // 4 == device, 1, 0)
                    pick = jnp.where(hit == 1, bodies[k], pick)
                    live = live + hit
                    free[k] = free[k] - hit
                    taken[k] = taken[k] + hit
                place = first * own + i * count + e
                chosen[2 * place] = pick
                chosen[2 * place + 1] = live
            first = first + count
        for k in range(slot_count):
            done[i, k] = taken[k]
        return 0

    lax.fori_loop(0, own, choose, 0)
    keep_done = pltpu.make_async_copy(done, done_out, store_sem)
    keep_done.start()

    target_stage(nodes, own, lambda c: own_geometry[c], centre, features)
    total[...] = jnp.zeros_like(total)
    worst[...] = jnp.full_like(worst, -1.0)
    for k in range(own * COMPS):
        slots[k] = jnp.full((8, LANES), FAR_AWAY if k % COMPS < 3 else 0.0, F32)
    kernel1[...] = jnp.zeros_like(kernel1)

    first_set = (kernel0, moment0, spread0)
    second_set = (kernel1, moment1, spread1)

    def early_pairs(phase, geometry, device):
        count = PHASES[phase]
        first = sum(PHASES[:phase])
        last = own * count - 1

        def source(m, spread, moment):
            now = jnp.minimum(m, last)
            i = now // count
            e = now % count
            place = first * own + now
            body = chosen[2 * place]
            live = chosen[2 * place + 1].astype(F32)
            base = 0 if device is not None else (body // 4) * COMPS
            raw = [geometry[base + c, pl.ds(body % 4, 1), :] for c in range(COMPS)]
            for c in range(3):
                slots[i * COMPS + c, pl.ds(first + e, 1), :] = raw[c]
                slots[i * COMPS + 3 + c, pl.ds(first + e, 1), :] = raw[3 + c] * live
            scale = live * jnp.where(m <= last, F32(1.0), F32(0.0))
            source_stage(raw, i, scale, centre, worst, spread, moment)

        def target_of(m):
            return jnp.clip(m, 0, last) // count

        near_pairs(last + 1, target_of, source, features, total, first_set, second_set)

    early_pairs(0, own_geometry, s)

    across_wait(0, own_geometry, s)
    partner_copy().wait_recv()
    across_start(1, partner_geometry, partner)
    for c in range(COMPS):
        row_geometry[s * COMPS + c] = own_geometry[c]
        row_geometry[partner * COMPS + c] = partner_geometry[c]

    early_pairs(1, partner_geometry, partner)

    for step in range(1, 8):
        remote(
            lists.at[s],
            lists.at[(s + 8 - step) % 8],
            list_send.at[step - 1],
            list_recv.at[step - 1],
            (t, partner),
        ).wait_recv()
    rows = 8 * own
    listed = lists[...].reshape(rows, 128)
    ids = s * 128 + lax.broadcasted_iota(jnp.int32, (rows, 128), 1)
    hit = ids == t * rows + lax.broadcasted_iota(jnp.int32, (rows, 128), 0)
    for k in range(slot_count):
        hit = jnp.logical_or(hit, ids == listed[:, k : k + 1])
    mask[...] = jnp.where(hit, F32(0.0), F32(1.0))

    def coef_arrival(k):
        return remote(
            coef_mine, coef_parts.at[k], coef_send.at[k], coef_recv.at[k], (t, partner)
        )

    every(lambda k: coef_arrival(k).wait_recv(), as_source)
    gathered = coef_parts[...].reshape(t_count, 128).astype(BF16)
    from_row = lax.broadcasted_iota(jnp.int32, (t_count, 128), 0)
    to_lane = lax.broadcasted_iota(jnp.int32, (t_count, 128), 1)
    coef = jnp.zeros((16, 128), F32)
    for j in range(own):
        chooser = jnp.where(to_lane == own * from_row + j, F32(1.0), F32(0.0)).astype(BF16)
        coef = coef + lax.dot_general(
            gathered[:, 16 * j : 16 * j + 16],
            chooser,
            (((0,), (0,)), ((), ())),
            preferred_element_type=F32,
        )
    loads[6].wait()

    def fold(i, _):
        kept = coef * mask[pl.ds(i, 1), :]
        product = held[i].astype(F32) * kept[None]
        folded[pl.ds(pl.multiple_of(i * 16, 16), 16), :] = jnp.sum(product, axis=1)
        return 0

    lax.fori_loop(0, rows, fold, 0)
    for q in range(4):
        turned = folded[q * 128 : (q + 1) * 128, :].T
        far_mine[q] = jnp.sum(turned, axis=0, keepdims=True)

    def far_copy(step):
        other = (s + step) % 8
        return remote(
            far_mine.at[other // 2],
            far_parts.at[step - 1],
            far_send.at[step - 1],
            far_recv.at[step - 1],
            (t, other),
        )

    for step in range(1, 8):
        far_copy(step).start()

    across_wait(1, partner_geometry, partner)
    partner_copy().wait_send()
    for step in range(1, 4):
        row_copy(0, step, own_geometry, s, partner).wait_send()
    for step in range(1, 8):
        list_copy(step).wait_send()
    every(lambda k: coef_copy(k).wait_send(), t)
    early_pairs(2, partner_geometry, partner)

    early_pairs(3, row_geometry, None)
    for i in range(own):
        sums = last_nodes(nodes, i, lambda c: own_geometry[c], slots)
        for c in range(3):
            empty = jnp.zeros((1, 128 + MAIN - nodes), F32)
            tails[c, i : i + 1, :] = jnp.concatenate([sums[c], empty], axis=1)

    for step in range(1, 8):
        far_copy(step).wait_recv()
    w = far_mine[s // 2]
    for step in range(1, 8):
        w = w + far_parts[step - 1]
    w = jnp.broadcast_to(w, (8, 128))
    coupled[...] = jnp.where(s % 2 == 1, pltpu.roll(w, 64, 1), w)


    for side in range(2):
        there = t > 0 if side == 0 else t < t_count - 1
        mine = t < t_count - 1 if side == 0 else t > 0
        columns = [
            ((s if index < 4 else partner) + 8 - 2 * (index % 4)) % 8 for index in range(8)
        ]

        @pl.when(there)
        def _():
            for index, column in enumerate(columns):
                halo_copy(side, index, own_geometry, column).wait_recv()

        @pl.when(mine)
        def _():
            for index, column in enumerate(columns):
                halo_copy(side, index, own_geometry, column).wait_send()

    for step in range(1, 4):
        row_copy(1, step, partner_geometry, partner, partner).wait_send()
    for step in range(1, 8):
        far_copy(step).wait_send()

    keep_done.wait()


def velocity_kernel(
    nodes,
    near_in,
    row_geometry,
    halo_geometry,
    coupled,
    early,
    early_worst,
    early_tail,
    done_in,
    basis_in,
    out,
    near,
    done,
    basis,
    used,
    places,
    centre,
    features,
    spread0,
    spread1,
    moment0,
    moment1,
    kernel0,
    kernel1,
    total,
    slots,
    worst,
    columns,
    load_sem,
):
    loads = [
        pltpu.make_async_copy(source, target, load_sem.at[index])
        for index, (source, target) in enumerate(
            (
                (near_in, near),
                (done_in, done),
                (basis_in, basis),
            )
        )
    ]
    for load in loads:
        load.start()
    t = lax.axis_index("tgt")
    s = lax.axis_index("src")
    own = out.shape[1]
    per_body = near.shape[1]
    total[...] = jnp.zeros_like(total)
    kernel1[...] = jnp.zeros_like(kernel1)
    target_stage(nodes, own, lambda c: row_geometry[s * COMPS + c], centre, features)

    for load in loads[:2]:
        load.wait()

    def listing(k, carry):
        n, taken = carry
        i = k // per_body
        slot = k % per_body
        taken = jnp.where(slot == 0, 0, taken)
        left = jnp.logical_and(near[i, slot] >= 0, done[i, slot] == 0)

        @pl.when(left)
        def _():
            used[n] = k
            places[n] = taken

        more = jnp.where(left, 1, 0)
        return n + more, taken + more

    n, _ = lax.fori_loop(0, own * per_body, listing, (jnp.int32(0), jnp.int32(0)))
    for k in range(2):
        used[n + k] = 0
        places[n + k] = 8

    worst[...] = early_worst[...]
    for k in range(own * COMPS):
        slots[k, 0:8] = jnp.full((8, LANES), FAR_AWAY if k % COMPS < 3 else 0.0, F32)

    def rows_of(body):
        inside = jnp.logical_and(body >= 0, body < 32)
        here = jnp.where(inside, body, 0)
        there = jnp.where(inside, 0, jnp.where(body < 0, body + 32, body))
        base = (here // 4) * COMPS
        halo = (there // 4) * COMPS
        place = body % 4
        return [
            jnp.where(
                inside,
                row_geometry[base + c, pl.ds(place, 1), :],
                halo_geometry[halo + c, pl.ds(place, 1), :],
            )
            for c in range(COMPS)
        ]

    def source(m, spread, moment):
        k = used[m]
        i = k // per_body
        raw = rows_of(near[i, k % per_body] - t * 32)
        live = jnp.where(m < n, F32(1.0), F32(0.0))
        for c in range(3):
            slots[i * COMPS + c, pl.ds(places[m], 1), :] = raw[c]
            slots[i * COMPS + 3 + c, pl.ds(places[m], 1), :] = raw[3 + c] * live
        source_stage(raw, i, live, centre, worst, spread, moment)

    near_pairs(
        n,
        lambda m: used[jnp.maximum(m, 0)] // per_body,
        source,
        features,
        total,
        (kernel0, moment0, spread0),
        (kernel1, moment1, spread1),
    )

    loads[2].wait()
    row8 = lax.broadcasted_iota(jnp.int32, (8, 128), 0)
    lane8 = lax.broadcasted_iota(jnp.int32, (8, 128), 1)
    diagonal = jnp.where(lane8 // 16 == row8, coupled[...], 0.0).astype(BF16)[:, :64]
    far = []
    for c in range(3):
        flat = jnp.concatenate([basis[i, c] for i in range(own)], axis=0)
        far.append(jnp.dot(diagonal, flat, preferred_element_type=F32))

    for i in range(own):
        sums = last_nodes(nodes, i, lambda c: row_geometry[s * COMPS + c], slots)
        for c in range(3):
            tail = sums[c] + early_tail[c, i : i + 1, 0 : nodes - MAIN]
            out[c, i : i + 1, MAIN:nodes] = tail + far[c][i : i + 1, MAIN:nodes]

    crowded = jnp.max(worst[...]) > 0.0

    @pl.when(jnp.logical_not(crowded))
    def _():
        for i in range(own):
            at = total[i] + early[i]
            g = at[0:16] + at[16:32] + at[32:48]
            x = [
                row_geometry[s * COMPS + c, i : i + 1, :MAIN] - centre[c, i : i + 1, :MAIN]
                for c in range(3)
            ]
            plain = [g[k : k + 1] for k in range(3)]
            first = [[g[b + k : b + k + 1] for k in range(3)] for b in (4, 8, 12)]
            last = [g[k : k + 1] for k in (7, 11, 15)]
            square = x[0] * x[0] + x[1] * x[1] + x[2] * x[2]
            inner = x[0] * plain[0] + x[1] * plain[1] + x[2] * plain[2] - g[3:4]
            for c in range(3):
                u = square * plain[c] + last[c] + x[c] * inner
                for k in range(3):
                    u = u - x[k] * (2.0 * first[k][c] + first[c][k])
                out[c, i : i + 1, :MAIN] = u + far[c][i : i + 1, :MAIN]

    @pl.when(crowded)
    def _():
        for i in range(own):
            for c in range(3):
                out[c, i : i + 1, :MAIN] = far[c][i : i + 1, :MAIN]

        def direct(k, _):
            i = k // per_body
            body = near[i, k % per_body]

            @pl.when(body >= 0)
            def _():
                empty = jnp.zeros((2, LANES), F32)
                rows = rows_of(body - t * 32)
                columns[...] = jnp.concatenate(rows + [empty], axis=0).T
                x = [row_geometry[s * COMPS + c, pl.ds(i, 1), :MAIN] for c in range(3)]

                def eight(q, sums):
                    block = columns[pl.ds(pl.multiple_of(q * 8, 8), 8), :]
                    d = [x[c] - block[:, c : c + 1] for c in range(3)]
                    w = [block[:, 3 + c : 4 + c] for c in range(3)]
                    inverse = lax.rsqrt(d[0] * d[0] + d[1] * d[1] + d[2] * d[2])
                    pull = d[0] * w[0] + d[1] * w[1] + d[2] * w[2]
                    pull = pull * (inverse * inverse * inverse)
                    return tuple(sums[c] + (w[c] * inverse + d[c] * pull) for c in range(3))

                start = tuple(jnp.zeros((8, MAIN), F32) for _ in range(3))
                sums = lax.fori_loop(0, ROWS // 8, eight, start)
                for c in range(3):
                    out[c, pl.ds(i, 1), :MAIN] += jnp.sum(sums[c], axis=0, keepdims=True)

            return 0

        lax.fori_loop(0, own * per_body, direct, 0)


def local(positions, weights, density, near_source, couplings, source_basis, target_basis):
    own, _, nodes = positions.shape
    vmem = pl.BlockSpec(memory_space=pltpu.VMEM)
    hbm = pl.BlockSpec(memory_space=pltpu.HBM)
    dma = pltpu.SemaphoreType.DMA
    turned = (1, 0, 2)
    centred = [
        pltpu.VMEM((4, own, LANES), F32),
        pltpu.VMEM((own, FACTORS, MAIN), BF16),
        pltpu.VMEM((FACTORS, ROWS), BF16),
        pltpu.VMEM((FACTORS, ROWS), BF16),
        pltpu.VMEM((MOMENTS, ROWS), BF16),
        pltpu.VMEM((MOMENTS, ROWS), BF16),
        pltpu.VMEM((ROWS, MAIN), BF16),
        pltpu.VMEM((ROWS, MAIN), BF16),
    ]
    moved = pl.pallas_call(
        functools.partial(exchange_kernel, nodes),
        out_shape=(
            pltpu.VMEM((8 * COMPS, own, LANES), F32),
            pltpu.VMEM((16 * COMPS, own, LANES), F32),
            pltpu.VMEM((8, 128), F32),
            pltpu.VMEM((own, MOMENTS, MAIN), F32),
            pltpu.VMEM((8, LANES), F32),
            pltpu.VMEM((3, own, 128), F32),
            pltpu.VMEM((own, 8), jnp.int32),
        ),
        in_specs=[hbm] * 6,
        out_specs=(vmem,) * 7,
        scratch_shapes=[
            pltpu.VMEM((COMPS, own, LANES), F32),
            pltpu.VMEM((COMPS, own, LANES), F32),
            pltpu.VMEM((own * COMPS, 8, LANES), F32),
            pltpu.VMEM((3, own, nodes), F32),
            pltpu.VMEM((own, nodes), F32),
            pltpu.VMEM((3, own, nodes), F32),
            pltpu.VMEM((own, 8), jnp.int32),
            pltpu.SMEM((own, 8), jnp.int32),
            pltpu.VMEM((32, 16, 16, 128), BF16),
            pltpu.VMEM((own, 3, 16, nodes), BF16),
            pltpu.VMEM((1, 128), F32),
            pltpu.VMEM((32, 1, 128), F32),
            pltpu.VMEM((8, own, 128), jnp.int32),
            pltpu.VMEM((32, 128), F32),
            pltpu.VMEM((512, 128), F32),
            pltpu.VMEM((4, 1, 128), F32),
            pltpu.VMEM((7, 1, 128), F32),
            pltpu.SMEM((2 * own * EARLY,), jnp.int32),
            pltpu.SMEM((own, 8), jnp.int32),
            *centred,
            dma((7,)),
            dma,
            dma((7,)),
            dma((7,)),
            dma((32,)),
            dma((32,)),
            dma((7,)),
            dma((7,)),
            dma((7,)),
            dma((7,)),
            dma((16,)),
            dma((16,)),
        ],
        compiler_params=pltpu.CompilerParams(
            collective_id=0, has_side_effects=True, vmem_limit_bytes=VMEM_BYTES
        ),
        name="exchange",
    )(
        positions.transpose(turned),
        weights,
        density.transpose(turned),
        near_source,
        couplings.transpose(0, 2, 3, 1),
        source_basis.transpose(0, 2, 1, 3),
    )
    out = pl.pallas_call(
        functools.partial(velocity_kernel, nodes),
        out_shape=jax.ShapeDtypeStruct((3, own, nodes), F32),
        in_specs=[hbm] + [vmem] * 7 + [hbm],
        out_specs=vmem,
        scratch_shapes=[
            pltpu.SMEM((own, 8), jnp.int32),
            pltpu.SMEM((own, 8), jnp.int32),
            pltpu.VMEM((own, 3, 16, nodes), BF16),
            pltpu.SMEM((40,), jnp.int32),
            pltpu.SMEM((40,), jnp.int32),
            *centred,
            pltpu.VMEM((own, MOMENTS, MAIN), F32),
            pltpu.VMEM((own * COMPS, 16, LANES), F32),
            pltpu.VMEM((8, LANES), F32),
            pltpu.VMEM((LANES, 8), F32),
            dma((3,)),
        ],
        compiler_params=pltpu.CompilerParams(vmem_limit_bytes=VMEM_BYTES // 2),
        name="velocity",
    )(
        near_source,
        *moved,
        target_basis.transpose(0, 2, 1, 3),
    )
    return out.transpose(turned)


def solution(mesh):
    placed = (
        P(("tgt", "src"), None, None),
        P(("tgt", "src"), None),
        P(("tgt", "src"), None, None),
        P(("tgt", "src"), None),
        P("tgt", "src", None, None),
        P(("tgt", "src"), None, None, None),
        P(("tgt", "src"), None, None, None),
    )
    return jax.shard_map(
        local, mesh=mesh, in_specs=placed, out_specs=P(("tgt", "src"), None, None), check_vma=False
    )
```

```python
import functools
import jax
import jax.numpy as jnp
from jax import lax
from jax.experimental import pallas as pl
from jax.experimental.pallas import tpu as pltpu
from jax.sharding import PartitionSpec as P

F32 = jnp.float32
BF16 = jnp.bfloat16
LANES = 768
ROWS = 656
MAIN = 640
COMPS = 6
TILES = MAIN // 128
BLOCK = COMPS * TILES + 1
FAR_AWAY = 1000.0
LEAST_GAP = 0.1
MOST_RATIO = 70.0
PHASES = (2, 1, 1, 1)
FACTORS = 32
MOMENTS = 48
EARLY = sum(PHASES)
CUTS = (0, 256, 512, ROWS)
VMEM_BYTES = 56 * 2**20
MESH = pl.DeviceIdType.MESH


def remote(source, target, send, recv, device):
    return pltpu.make_async_remote_copy(
        src_ref=source,
        dst_ref=target,
        send_sem=send,
        recv_sem=recv,
        device_id=device,
        device_id_type=MESH,
    )


def turn_lanes(value, shift):
    rows = value.shape[0]
    filled = jnp.concatenate([value, jnp.zeros((8 - rows, 128), F32)], axis=0)
    return pltpu.roll(filled, shift % 128, 1)[:rows]


def body_rows(nodes, tile):
    last = tile(COMPS * TILES)
    lane = lax.broadcasted_iota(jnp.int32, last.shape, 1)
    width = nodes - MAIN
    rows = []
    for c in range(COMPS):
        tail = turn_lanes(last, -width * c) if c else last
        tail = jnp.where(lane < width, tail, FAR_AWAY if c < 3 else 0.0)
        rows.append(jnp.concatenate([tile(c * TILES + k) for k in range(TILES)] + [tail], axis=1))
    return rows


def split(value):
    high = value.astype(BF16).astype(F32)
    rest = value - high
    middle = rest.astype(BF16).astype(F32)
    return high, middle, rest - middle


def by_quad(sub, first, second, third, fourth):
    quad = sub % 4
    return jnp.where(
        quad == 0, first, jnp.where(quad == 1, second, jnp.where(quad == 2, third, fourth))
    )


def target_stage(nodes, own, bodies, centre, features):
    inside = lax.broadcasted_iota(jnp.int32, (own, LANES), 1) < nodes
    radius = jnp.zeros((own, LANES), F32)
    offsets = []
    for c in range(3):
        value = bodies[c]
        mean = jnp.sum(jnp.where(inside, value, 0.0), axis=1, keepdims=True) / nodes
        centre[c] = jnp.broadcast_to(mean, (own, LANES))
        offset = jnp.where(inside, value - mean, 0.0)
        offsets.append(offset)
        radius = radius + offset * offset
    largest = jnp.max(radius, axis=1, keepdims=True)
    centre[3] = jnp.broadcast_to(jnp.sqrt(largest), (own, LANES))
    sub = lax.broadcasted_iota(jnp.int32, (8, LANES), 0)
    for i in range(own):
        x = [jnp.broadcast_to(offset[i : i + 1, :], (8, LANES)) for offset in offsets]
        square = jnp.broadcast_to(radius[i : i + 1, :], (8, LANES))
        high, middle, low = split(by_quad(sub, x[0], x[1], x[2], square))
        one = jnp.ones_like(square)
        stack = [
            jnp.where(sub % 4 == 3, one, jnp.where(sub < 4, high, middle)),
            jnp.where(sub < 3, low, jnp.where(sub == 3, one, high)),
            jnp.where(sub < 4, middle, jnp.where(sub == 7, low, high)),
            jnp.zeros_like(square),
        ]
        features[i] = jnp.concatenate(stack, axis=0).astype(BF16)[:, :MAIN]


def source_stage(raw, i, live, centre, worst, spread, moment):
    sub = lax.broadcasted_iota(jnp.int32, (8, LANES), 0)
    y = [jnp.broadcast_to(raw[c] - centre[c, pl.ds(i, 1), :], (8, LANES)) for c in range(3)]
    w = [jnp.broadcast_to(raw[3 + c], (8, LANES)) for c in range(3)]
    square = y[0] * y[0] + y[1] * y[1] + y[2] * y[2]
    reach = jnp.sqrt(square)
    size = jnp.broadcast_to(centre[3, pl.ds(i, 1), :], (8, LANES))
    ratio = (reach + size) - MOST_RATIO * jnp.maximum(reach - size, LEAST_GAP)
    worst[...] = jnp.maximum(worst[...], ratio)
    high, middle, low = split(by_quad(sub, -2.0 * y[0], -2.0 * y[1], -2.0 * y[2], square))
    one = jnp.ones_like(square)
    stack = [
        jnp.where(sub == 7, middle, high),
        jnp.where(sub < 3, high, jnp.where(sub == 3, low, jnp.where(sub == 7, one, middle))),
        jnp.where(sub % 4 == 3, one, jnp.where(sub < 4, middle, low)),
        jnp.zeros_like(square),
    ]
    spread[...] = jnp.concatenate(stack, axis=0).astype(BF16)[:, :ROWS]
    w = [live * value for value in w]
    along = y[0] * w[0] + y[1] * w[1] + y[2] * w[2]
    plain = by_quad(sub, w[0], w[1], w[2], one)
    last = [w[c] * square + along * y[c] for c in range(3)]
    front = plain * jnp.where(sub < 4, one, y[0])
    front = jnp.where(sub == 3, along, jnp.where(sub == 7, last[0], front))
    back = plain * jnp.where(sub < 4, y[1], y[2])
    back = jnp.where(sub == 3, last[1], jnp.where(sub == 7, last[2], back))
    fronts, backs = split(front), split(back)
    stack = [value for pair in zip(fronts, backs) for value in pair]
    moment[...] = jnp.concatenate(stack, axis=0).astype(BF16)[:, :ROWS]


def last_nodes(nodes, i, bodies, slots):
    y = [slots[i * COMPS + c, 0:8] for c in range(3)]
    w = [slots[i * COMPS + 3 + c, 0:8] for c in range(3)]
    sums = [[], [], []]
    for node in range(MAIN, nodes):
        d = [bodies[c][i : i + 1, node : node + 1] - y[c] for c in range(3)]
        inverse = lax.rsqrt(d[0] * d[0] + d[1] * d[1] + d[2] * d[2])
        pull = (d[0] * w[0] + d[1] * w[1] + d[2] * w[2]) * (inverse * inverse * inverse)
        for c in range(3):
            summed = jnp.sum(w[c] * inverse + d[c] * pull, axis=0, keepdims=True)
            sums[c].append(jnp.sum(summed, axis=1, keepdims=True))
    return [jnp.concatenate(values, axis=1) for values in sums]


def kernel_chunk(features, spread, kernel, low, high):
    squared = lax.dot_general(
        spread[:, low:high], features, (((0,), (0,)), ((), ())), preferred_element_type=F32
    )
    inverse = lax.rsqrt(squared)
    kernel[low:high] = (inverse * inverse * inverse).astype(BF16)


def moment_chunk(kernel, moment, low, high):
    return jnp.dot(moment[:, low:high], kernel[low:high], preferred_element_type=F32)


def near_pairs(count, target_of, source, features, total, first, second):
    def turn(q, _):
        for e, (mine, other) in enumerate(((first, second), (second, first))):
            m = 2 * q + e
            for low, high in zip(CUTS[:-1], CUTS[1:]):
                kernel_chunk(features[target_of(m)], mine[2], mine[0], low, high)
                total[target_of(m - 1)] += moment_chunk(other[0], other[1], low, high)
            source(m + 1, other[2], other[1])
        return 0

    halves = (count + 1) // 2
    second[1][...] = jnp.zeros_like(second[1])
    source(0, first[2], first[1])
    lax.fori_loop(0, halves, turn, 0)
    total[target_of(2 * halves - 1)] += moment_chunk(second[0], second[1], 0, ROWS)


def exchange_kernel(
    nodes,
    positions_in,
    weights_in,
    density_in,
    near_in,
    couplings_in,
    basis_in,
    row_geometry,
    halo_geometry,
    coupled,
    total,
    worst,
    tails,
    done_out,
    own_geometry,
    partner_geometry,
    slots,
    positions,
    weights,
    density,
    near,
    near_scalar,
    held,
    basis,
    coef_mine,
    coef_parts,
    lists,
    mask,
    folded,
    far_mine,
    far_parts,
    chosen,
    done,
    centre,
    features,
    spread0,
    spread1,
    moment0,
    moment1,
    kernel0,
    kernel1,
    load_sem,
    store_sem,
    list_send,
    list_recv,
    coef_send,
    coef_recv,
    far_send,
    far_recv,
    row_send,
    row_recv,
    halo_send,
    halo_recv,
):
    t = lax.axis_index("tgt")
    s = lax.axis_index("src")
    t_count = lax.axis_size("tgt")
    quarter = t // 4
    own = positions.shape[1]
    slot_count = near.shape[1]
    loops_back = quarter == s
    partner = s + 1 - 2 * (s % 2)

    loads = [
        pltpu.make_async_copy(source, target, load_sem.at[index])
        for index, (source, target) in enumerate(
            (
                (positions_in, positions),
                (weights_in, weights),
                (density_in, density),
                (near_in, near),
                (near_in, near_scalar),
                (basis_in, basis),
                (couplings_in, held),
            )
        )
    ]
    for load in loads:
        load.start()

    barrier = pltpu.get_barrier_semaphore()

    def greet(device):
        pl.semaphore_signal(barrier, inc=1, device_id=device, device_id_type=MESH)

    for step in range(1, 8):
        greet((t, (s + step) % 8))

    def every(act, mine):
        for k in range(t_count - 1):
            act(k + jnp.where(jnp.logical_and(loops_back, mine <= k), 1, 0))

        @pl.when(jnp.logical_not(loops_back))
        def _():
            act(t_count - 1)

    as_source = (t % 4) * 8 + s

    @pl.when(t > 0)
    def _():
        greet((t - 1, s))

    @pl.when(t < t_count - 1)
    def _():
        greet((t + 1, s))

    every(lambda k: greet((4 * s + k // 8, k % 8)), as_source)

    def block(column):
        return row_geometry.at[pl.ds(column * BLOCK, BLOCK)]

    for load in loads[:4]:
        load.wait()
    pad = jnp.zeros((own, LANES - nodes), F32)
    tails_mine = jnp.zeros((own, 128), F32)
    for c in range(COMPS):
        value = positions[c] if c < 3 else density[c - 3] * weights[...]
        value = jnp.concatenate([value, pad], axis=1)
        for k in range(TILES):
            own_geometry[c * TILES + k] = value[:, 128 * k : 128 * k + 128]
        tails_mine = tails_mine + turn_lanes(value[:, MAIN:], (nodes - MAIN) * c)
    own_geometry[COMPS * TILES] = tails_mine
    lists[s] = jnp.concatenate([near[...], jnp.full((own, 120), -1, jnp.int32)], axis=1)

    loads[5].wait()
    sub16 = lax.broadcasted_iota(jnp.int32, (16, 128), 0)
    lane16 = lax.broadcasted_iota(jnp.int32, (16, 128), 1)
    spread = jnp.zeros((16, 128), F32)
    for j in range(own):
        product = basis[j, 0].astype(F32) * density[0, j : j + 1, :]
        for c in range(1, 3):
            product = product + basis[j, c].astype(F32) * density[c, j : j + 1, :]
        value = jnp.sum(product, axis=1, keepdims=True)
        spread = jnp.where(lane16 == sub16 + 16 * j, value, spread)
    coef_mine[...] = jnp.sum(spread, axis=0, keepdims=True).astype(BF16).astype(F32)

    loads[4].wait()

    def choose(i, _):
        bodies = [near_scalar[i, k] - t * 32 for k in range(slot_count)]
        free = [jnp.where(body >= 0, 1, 0) * jnp.where(body < 32, 1, 0) for body in bodies]
        taken = [jnp.int32(0)] * slot_count
        first = 0
        for phase, count in enumerate(PHASES):
            device = (s, partner, partner, None)[phase]
            other = s * 4 + (i + 1) % own if phase in (0, 3) else partner * 4
            for e in range(count):
                pick = jnp.int32(0) + other
                live = jnp.int32(0)
                for k in range(slot_count):
                    hit = free[k] * (1 - live)
                    if device is not None:
                        hit = hit * jnp.where(bodies[k] // 4 == device, 1, 0)
                    pick = jnp.where(hit == 1, bodies[k], pick)
                    live = live + hit
                    free[k] = free[k] - hit
                    taken[k] = taken[k] + hit
                place = first * own + i * count + e
                chosen[2 * place] = pick
                chosen[2 * place + 1] = live
            first = first + count
        for k in range(slot_count):
            done[i, k] = taken[k]
        return 0

    lax.fori_loop(0, own, choose, 0)
    keep_done = pltpu.make_async_copy(done, done_out, store_sem)
    keep_done.start()

    bodies = body_rows(nodes, lambda k: own_geometry[k])
    target_stage(nodes, own, bodies, centre, features)
    total[...] = jnp.zeros_like(total)
    worst[...] = jnp.full_like(worst, -1.0)
    for k in range(own * COMPS):
        slots[k] = jnp.full((8, LANES), FAR_AWAY if k % COMPS < 3 else 0.0, F32)
    kernel1[...] = jnp.zeros_like(kernel1)

    pl.semaphore_wait(
        barrier,
        7
        + t_count
        - jnp.where(loops_back, 1, 0)
        + jnp.where(t > 0, 1, 0)
        + jnp.where(t < t_count - 1, 1, 0),
    )

    def partner_copy():
        return remote(
            own_geometry, partner_geometry, row_send.at[0], row_recv.at[0], (t, partner)
        )

    def row_copy(turn, step, source, column, device):
        return remote(
            source,
            block(column),
            row_send.at[turn * 3 + step],
            row_recv.at[turn * 3 + step],
            (t, device),
        )

    def halo_copy(side, index, source, column):
        return remote(
            source,
            halo_geometry.at[pl.ds((side * 8 + column) * BLOCK, BLOCK)],
            halo_send.at[side * 8 + index],
            halo_recv.at[side * 8 + index],
            (t + 1 - 2 * side, s),
        )

    def halo_start(index, source, column):
        @pl.when(t < t_count - 1)
        def _():
            halo_copy(0, index, source, column).start()

        @pl.when(t > 0)
        def _():
            halo_copy(1, index, source, column).start()

    def across_start(turn, source, column):
        for step in range(1, 4):
            row_copy(turn, step, source, column, (s + 2 * step) % 8).start()
        halo_start(4 * turn, source, column)

    def across_wait(turn, source, column):
        for step in range(1, 4):
            here = (column + 8 - 2 * step) % 8
            row_copy(turn, step, source, here, partner).wait_recv()
            halo_start(4 * turn + step, block(here), here)

    def coef_copy(k):
        return remote(
            coef_mine,
            coef_parts.at[(t % 4) * 8 + s],
            coef_send.at[k],
            coef_recv.at[(t % 4) * 8 + s],
            (k, quarter),
        )

    def list_copy(step):
        return remote(
            lists.at[s],
            lists.at[s],
            list_send.at[step - 1],
            list_recv.at[step - 1],
            (t, (s + step) % 8),
        )

    partner_copy().start()
    every(lambda k: coef_copy(k).start(), t)
    across_start(0, own_geometry, s)
    for step in range(1, 8):
        list_copy(step).start()

    @pl.when(loops_back)
    def _():
        coef_parts[(t % 4) * 8 + s] = coef_mine[...]

    first_set = (kernel0, moment0, spread0)
    second_set = (kernel1, moment1, spread1)

    def early_pairs(phase, geometry, device):
        count = PHASES[phase]
        first = sum(PHASES[:phase])
        last = own * count - 1

        def source(m, spread, moment):
            now = jnp.minimum(m, last)
            i = now // count
            e = now % count
            place = first * own + now
            body = chosen[2 * place]
            live = chosen[2 * place + 1].astype(F32)
            base = 0 if device is not None else (body // 4) * BLOCK
            raw = body_rows(nodes, lambda k: geometry[base + k, pl.ds(body % 4, 1), :])
            for c in range(3):
                slots[i * COMPS + c, pl.ds(first + e, 1), :] = raw[c]
                slots[i * COMPS + 3 + c, pl.ds(first + e, 1), :] = raw[3 + c] * live
            scale = live * jnp.where(m <= last, F32(1.0), F32(0.0))
            source_stage(raw, i, scale, centre, worst, spread, moment)

        def target_of(m):
            return jnp.clip(m, 0, last) // count

        near_pairs(last + 1, target_of, source, features, total, first_set, second_set)

    early_pairs(0, own_geometry, s)

    across_wait(0, own_geometry, s)
    partner_copy().wait_recv()
    across_start(1, partner_geometry, partner)
    for k in range(BLOCK):
        row_geometry[s * BLOCK + k] = own_geometry[k]
        row_geometry[partner * BLOCK + k] = partner_geometry[k]

    early_pairs(1, partner_geometry, partner)

    for step in range(1, 8):
        remote(
            lists.at[s],
            lists.at[(s + 8 - step) % 8],
            list_send.at[step - 1],
            list_recv.at[step - 1],
            (t, partner),
        ).wait_recv()
    rows = 8 * own
    listed = lists[...].reshape(rows, 128)
    ids = s * 128 + lax.broadcasted_iota(jnp.int32, (rows, 128), 1)
    hit = ids == t * rows + lax.broadcasted_iota(jnp.int32, (rows, 128), 0)
    for k in range(slot_count):
        hit = jnp.logical_or(hit, ids == listed[:, k : k + 1])
    mask[...] = jnp.where(hit, F32(0.0), F32(1.0))

    def coef_arrival(k):
        return remote(
            coef_mine, coef_parts.at[k], coef_send.at[k], coef_recv.at[k], (t, partner)
        )

    every(lambda k: coef_arrival(k).wait_recv(), as_source)
    gathered = coef_parts[...].reshape(t_count, 128).astype(BF16)
    from_row = lax.broadcasted_iota(jnp.int32, (t_count, 128), 0)
    to_lane = lax.broadcasted_iota(jnp.int32, (t_count, 128), 1)
    coef = jnp.zeros((16, 128), F32)
    for j in range(own):
        chooser = jnp.where(to_lane == own * from_row + j, F32(1.0), F32(0.0)).astype(BF16)
        coef = coef + lax.dot_general(
            gathered[:, 16 * j : 16 * j + 16],
            chooser,
            (((0,), (0,)), ((), ())),
            preferred_element_type=F32,
        )
    loads[6].wait()

    def fold(i, _):
        kept = coef * mask[pl.ds(i, 1), :]
        product = held[i].astype(F32) * kept[None]
        folded[pl.ds(pl.multiple_of(i * 16, 16), 16), :] = jnp.sum(product, axis=1)
        return 0

    lax.fori_loop(0, rows, fold, 0)
    for q in range(4):
        turned = folded[q * 128 : (q + 1) * 128, :].T
        far_mine[q] = jnp.sum(turned, axis=0, keepdims=True)

    def far_copy(step):
        other = (s + step) % 8
        return remote(
            far_mine.at[other // 2],
            far_parts.at[step - 1],
            far_send.at[step - 1],
            far_recv.at[step - 1],
            (t, other),
        )

    for step in range(1, 8):
        far_copy(step).start()

    across_wait(1, partner_geometry, partner)
    partner_copy().wait_send()
    for step in range(1, 4):
        row_copy(0, step, own_geometry, s, partner).wait_send()
    for step in range(1, 8):
        list_copy(step).wait_send()
    every(lambda k: coef_copy(k).wait_send(), t)
    early_pairs(2, partner_geometry, partner)

    early_pairs(3, row_geometry, None)
    for i in range(own):
        sums = last_nodes(nodes, i, bodies, slots)
        for c in range(3):
            empty = jnp.zeros((1, 128 + MAIN - nodes), F32)
            tails[c, i : i + 1, :] = jnp.concatenate([sums[c], empty], axis=1)

    for step in range(1, 8):
        far_copy(step).wait_recv()
    w = far_mine[s // 2]
    for step in range(1, 8):
        w = w + far_parts[step - 1]
    w = jnp.broadcast_to(w, (8, 128))
    coupled[...] = jnp.where(s % 2 == 1, pltpu.roll(w, 64, 1), w)


    for side in range(2):
        there = t > 0 if side == 0 else t < t_count - 1
        mine = t < t_count - 1 if side == 0 else t > 0
        columns = [
            ((s if index < 4 else partner) + 8 - 2 * (index % 4)) % 8 for index in range(8)
        ]

        @pl.when(there)
        def _():
            for index, column in enumerate(columns):
                halo_copy(side, index, own_geometry, column).wait_recv()

        @pl.when(mine)
        def _():
            for index, column in enumerate(columns):
                halo_copy(side, index, own_geometry, column).wait_send()

    for step in range(1, 4):
        row_copy(1, step, partner_geometry, partner, partner).wait_send()
    for step in range(1, 8):
        far_copy(step).wait_send()

    keep_done.wait()


def velocity_kernel(
    nodes,
    near_in,
    row_geometry,
    halo_geometry,
    coupled,
    early,
    early_worst,
    early_tail,
    done_in,
    basis_in,
    out,
    near,
    done,
    basis,
    used,
    places,
    centre,
    features,
    spread0,
    spread1,
    moment0,
    moment1,
    kernel0,
    kernel1,
    total,
    slots,
    worst,
    columns,
    load_sem,
):
    loads = [
        pltpu.make_async_copy(source, target, load_sem.at[index])
        for index, (source, target) in enumerate(
            (
                (near_in, near),
                (done_in, done),
                (basis_in, basis),
            )
        )
    ]
    for load in loads:
        load.start()
    t = lax.axis_index("tgt")
    s = lax.axis_index("src")
    own = out.shape[1]
    per_body = near.shape[1]
    total[...] = jnp.zeros_like(total)
    kernel1[...] = jnp.zeros_like(kernel1)
    bodies = body_rows(nodes, lambda k: row_geometry[s * BLOCK + k])
    target_stage(nodes, own, bodies, centre, features)

    for load in loads[:2]:
        load.wait()

    def listing(k, carry):
        n, taken = carry
        i = k // per_body
        slot = k % per_body
        taken = jnp.where(slot == 0, 0, taken)
        left = jnp.logical_and(near[i, slot] >= 0, done[i, slot] == 0)

        used[n] = k
        places[n] = taken
        more = jnp.where(left, 1, 0)
        return n + more, taken + more

    n, _ = lax.fori_loop(0, own * per_body, listing, (jnp.int32(0), jnp.int32(0)))
    for k in range(2):
        used[n + k] = 0
        places[n + k] = 8

    worst[...] = early_worst[...]
    for k in range(own * COMPS):
        slots[k, 0:8] = jnp.full((8, LANES), FAR_AWAY if k % COMPS < 3 else 0.0, F32)

    def rows_of(body):
        inside = jnp.logical_and(body >= 0, body < 32)
        here = jnp.where(inside, body, 0)
        there = jnp.where(inside, 0, jnp.where(body < 0, body + 32, body))
        base = (here // 4) * BLOCK
        halo = (there // 4) * BLOCK
        place = body % 4
        return body_rows(
            nodes,
            lambda k: jnp.where(
                inside,
                row_geometry[base + k, pl.ds(place, 1), :],
                halo_geometry[halo + k, pl.ds(place, 1), :],
            ),
        )

    def source(m, spread, moment):
        k = used[m]
        i = k // per_body
        raw = rows_of(near[i, k % per_body] - t * 32)
        live = jnp.where(m < n, F32(1.0), F32(0.0))
        for c in range(3):
            slots[i * COMPS + c, pl.ds(places[m], 1), :] = raw[c]
            slots[i * COMPS + 3 + c, pl.ds(places[m], 1), :] = raw[3 + c] * live
        source_stage(raw, i, live, centre, worst, spread, moment)

    near_pairs(
        n,
        lambda m: used[jnp.maximum(m, 0)] // per_body,
        source,
        features,
        total,
        (kernel0, moment0, spread0),
        (kernel1, moment1, spread1),
    )

    loads[2].wait()
    row8 = lax.broadcasted_iota(jnp.int32, (8, 128), 0)
    lane8 = lax.broadcasted_iota(jnp.int32, (8, 128), 1)
    diagonal = jnp.where(lane8 // 16 == row8, coupled[...], 0.0).astype(BF16)[:, :64]
    far = []
    for c in range(3):
        flat = jnp.concatenate([basis[i, c] for i in range(own)], axis=0)
        far.append(jnp.dot(diagonal, flat, preferred_element_type=F32))

    for i in range(own):
        sums = last_nodes(nodes, i, bodies, slots)
        for c in range(3):
            tail = sums[c] + early_tail[c, i : i + 1, 0 : nodes - MAIN]
            out[c, i : i + 1, MAIN:nodes] = tail + far[c][i : i + 1, MAIN:nodes]

    crowded = jnp.max(worst[...]) > 0.0

    @pl.when(jnp.logical_not(crowded))
    def _():
        for i in range(own):
            at = total[i] + early[i]
            g = at[0:16] + at[16:32] + at[32:48]
            x = [
                bodies[c][i : i + 1, :MAIN] - centre[c, i : i + 1, :MAIN] for c in range(3)
            ]
            plain = [g[k : k + 1] for k in range(3)]
            first = [[g[b + k : b + k + 1] for k in range(3)] for b in (4, 8, 12)]
            last = [g[k : k + 1] for k in (7, 11, 15)]
            square = x[0] * x[0] + x[1] * x[1] + x[2] * x[2]
            inner = x[0] * plain[0] + x[1] * plain[1] + x[2] * plain[2] - g[3:4]
            for c in range(3):
                u = square * plain[c] + last[c] + x[c] * inner
                for k in range(3):
                    u = u - x[k] * (2.0 * first[k][c] + first[c][k])
                out[c, i : i + 1, :MAIN] = u + far[c][i : i + 1, :MAIN]

    @pl.when(crowded)
    def _():
        for i in range(own):
            for c in range(3):
                out[c, i : i + 1, :MAIN] = far[c][i : i + 1, :MAIN]

        def direct(k, _):
            i = k // per_body
            body = near[i, k % per_body]

            @pl.when(body >= 0)
            def _():
                empty = jnp.zeros((2, LANES), F32)
                rows = rows_of(body - t * 32)
                columns[...] = jnp.concatenate(rows + [empty], axis=0).T
                x = [
                    jnp.concatenate(
                        [
                            row_geometry[s * BLOCK + c * TILES + k, pl.ds(i, 1), :]
                            for k in range(TILES)
                        ],
                        axis=1,
                    )
                    for c in range(3)
                ]

                def eight(q, sums):
                    block = columns[pl.ds(pl.multiple_of(q * 8, 8), 8), :]
                    d = [x[c] - block[:, c : c + 1] for c in range(3)]
                    w = [block[:, 3 + c : 4 + c] for c in range(3)]
                    inverse = lax.rsqrt(d[0] * d[0] + d[1] * d[1] + d[2] * d[2])
                    pull = d[0] * w[0] + d[1] * w[1] + d[2] * w[2]
                    pull = pull * (inverse * inverse * inverse)
                    return tuple(sums[c] + (w[c] * inverse + d[c] * pull) for c in range(3))

                start = tuple(jnp.zeros((8, MAIN), F32) for _ in range(3))
                sums = lax.fori_loop(0, ROWS // 8, eight, start)
                for c in range(3):
                    out[c, pl.ds(i, 1), :MAIN] += jnp.sum(sums[c], axis=0, keepdims=True)

            return 0

        lax.fori_loop(0, own * per_body, direct, 0)


def local(positions, weights, density, near_source, couplings, source_basis, target_basis):
    own, _, nodes = positions.shape
    vmem = pl.BlockSpec(memory_space=pltpu.VMEM)
    hbm = pl.BlockSpec(memory_space=pltpu.HBM)
    dma = pltpu.SemaphoreType.DMA
    turned = (1, 0, 2)
    centred = [
        pltpu.VMEM((4, own, LANES), F32),
        pltpu.VMEM((own, FACTORS, MAIN), BF16),
        pltpu.VMEM((FACTORS, ROWS), BF16),
        pltpu.VMEM((FACTORS, ROWS), BF16),
        pltpu.VMEM((MOMENTS, ROWS), BF16),
        pltpu.VMEM((MOMENTS, ROWS), BF16),
        pltpu.VMEM((ROWS, MAIN), BF16),
        pltpu.VMEM((ROWS, MAIN), BF16),
    ]
    moved = pl.pallas_call(
        functools.partial(exchange_kernel, nodes),
        out_shape=(
            pltpu.VMEM((8 * BLOCK, own, 128), F32),
            pltpu.VMEM((16 * BLOCK, own, 128), F32),
            pltpu.VMEM((8, 128), F32),
            pltpu.VMEM((own, MOMENTS, MAIN), F32),
            pltpu.VMEM((8, LANES), F32),
            pltpu.VMEM((3, own, 128), F32),
            pltpu.VMEM((own, 8), jnp.int32),
        ),
        in_specs=[hbm] * 6,
        out_specs=(vmem,) * 7,
        scratch_shapes=[
            pltpu.VMEM((BLOCK, own, 128), F32),
            pltpu.VMEM((BLOCK, own, 128), F32),
            pltpu.VMEM((own * COMPS, 8, LANES), F32),
            pltpu.VMEM((3, own, nodes), F32),
            pltpu.VMEM((own, nodes), F32),
            pltpu.VMEM((3, own, nodes), F32),
            pltpu.VMEM((own, 8), jnp.int32),
            pltpu.SMEM((own, 8), jnp.int32),
            pltpu.VMEM((32, 16, 16, 128), BF16),
            pltpu.VMEM((own, 3, 16, nodes), BF16),
            pltpu.VMEM((1, 128), F32),
            pltpu.VMEM((32, 1, 128), F32),
            pltpu.VMEM((8, own, 128), jnp.int32),
            pltpu.VMEM((32, 128), F32),
            pltpu.VMEM((512, 128), F32),
            pltpu.VMEM((4, 1, 128), F32),
            pltpu.VMEM((7, 1, 128), F32),
            pltpu.SMEM((2 * own * EARLY,), jnp.int32),
            pltpu.SMEM((own, 8), jnp.int32),
            *centred,
            dma((7,)),
            dma,
            dma((7,)),
            dma((7,)),
            dma((32,)),
            dma((32,)),
            dma((7,)),
            dma((7,)),
            dma((7,)),
            dma((7,)),
            dma((16,)),
            dma((16,)),
        ],
        compiler_params=pltpu.CompilerParams(
            collective_id=0, has_side_effects=True, vmem_limit_bytes=VMEM_BYTES
        ),
        name="exchange",
    )(
        positions.transpose(turned),
        weights,
        density.transpose(turned),
        near_source,
        couplings.transpose(0, 2, 3, 1),
        source_basis.transpose(0, 2, 1, 3),
    )
    out = pl.pallas_call(
        functools.partial(velocity_kernel, nodes),
        out_shape=jax.ShapeDtypeStruct((3, own, nodes), F32),
        in_specs=[hbm] + [vmem] * 7 + [hbm],
        out_specs=vmem,
        scratch_shapes=[
            pltpu.SMEM((own, 8), jnp.int32),
            pltpu.SMEM((own, 8), jnp.int32),
            pltpu.VMEM((own, 3, 16, nodes), BF16),
            pltpu.SMEM((40,), jnp.int32),
            pltpu.SMEM((40,), jnp.int32),
            *centred,
            pltpu.VMEM((own, MOMENTS, MAIN), F32),
            pltpu.VMEM((own * COMPS, 16, LANES), F32),
            pltpu.VMEM((8, LANES), F32),
            pltpu.VMEM((LANES, 8), F32),
            dma((3,)),
        ],
        compiler_params=pltpu.CompilerParams(vmem_limit_bytes=VMEM_BYTES // 2),
        name="velocity",
    )(
        near_source,
        *moved,
        target_basis.transpose(0, 2, 1, 3),
    )
    return out.transpose(turned)


def solution(mesh):
    placed = (
        P(("tgt", "src"), None, None),
        P(("tgt", "src"), None),
        P(("tgt", "src"), None, None),
        P(("tgt", "src"), None),
        P("tgt", "src", None, None),
        P(("tgt", "src"), None, None, None),
        P(("tgt", "src"), None, None, None),
    )
    return jax.shard_map(
        local, mesh=mesh, in_specs=placed, out_specs=P(("tgt", "src"), None, None), check_vma=False
    )
```

```python
import functools
import jax
import jax.numpy as jnp
from jax import lax
from jax.experimental import pallas as pl
from jax.experimental.pallas import tpu as pltpu
from jax.sharding import PartitionSpec as P

F32 = jnp.float32
BF16 = jnp.bfloat16
LANES = 768
ROWS = 656
MAIN = 640
COMPS = 6
TILES = MAIN // 128
BLOCK = COMPS * TILES + 1
FAR_AWAY = 1000.0
LEAST_GAP = 0.1
MOST_RATIO = 70.0
PHASES = (2, 1, 1, 1)
FACTORS = 32
MOMENTS = 48
EARLY = sum(PHASES)
CUTS = (0, 256, 512, ROWS)
VMEM_BYTES = 56 * 2**20
MESH = pl.DeviceIdType.MESH


def remote(source, target, send, recv, device):
    return pltpu.make_async_remote_copy(
        src_ref=source,
        dst_ref=target,
        send_sem=send,
        recv_sem=recv,
        device_id=device,
        device_id_type=MESH,
    )


def turn_lanes(value, shift):
    rows = value.shape[0]
    filled = jnp.concatenate([value, jnp.zeros((8 - rows, 128), F32)], axis=0)
    return pltpu.roll(filled, shift % 128, 1)[:rows]


def body_rows(nodes, tile):
    last = tile(COMPS * TILES)
    lane = lax.broadcasted_iota(jnp.int32, last.shape, 1)
    width = nodes - MAIN
    rows = []
    for c in range(COMPS):
        tail = turn_lanes(last, -width * c) if c else last
        tail = jnp.where(lane < width, tail, FAR_AWAY if c < 3 else 0.0)
        rows.append(jnp.concatenate([tile(c * TILES + k) for k in range(TILES)] + [tail], axis=1))
    return rows


def split(value):
    high = value.astype(BF16).astype(F32)
    rest = value - high
    middle = rest.astype(BF16).astype(F32)
    return high, middle, rest - middle


def by_quad(sub, first, second, third, fourth):
    quad = sub % 4
    return jnp.where(
        quad == 0, first, jnp.where(quad == 1, second, jnp.where(quad == 2, third, fourth))
    )


def target_stage(nodes, own, bodies, centre, features):
    inside = lax.broadcasted_iota(jnp.int32, (own, LANES), 1) < nodes
    radius = jnp.zeros((own, LANES), F32)
    offsets = []
    for c in range(3):
        value = bodies[c]
        mean = jnp.sum(jnp.where(inside, value, 0.0), axis=1, keepdims=True) / nodes
        centre[c] = jnp.broadcast_to(mean, (own, LANES))
        offset = jnp.where(inside, value - mean, 0.0)
        offsets.append(offset)
        radius = radius + offset * offset
    largest = jnp.max(radius, axis=1, keepdims=True)
    centre[3] = jnp.broadcast_to(jnp.sqrt(largest), (own, LANES))
    sub = lax.broadcasted_iota(jnp.int32, (8, LANES), 0)
    for i in range(own):
        x = [jnp.broadcast_to(offset[i : i + 1, :], (8, LANES)) for offset in offsets]
        square = jnp.broadcast_to(radius[i : i + 1, :], (8, LANES))
        high, middle, low = split(by_quad(sub, x[0], x[1], x[2], square))
        one = jnp.ones_like(square)
        stack = [
            jnp.where(sub % 4 == 3, one, jnp.where(sub < 4, high, middle)),
            jnp.where(sub < 3, low, jnp.where(sub == 3, one, high)),
            jnp.where(sub < 4, middle, jnp.where(sub == 7, low, high)),
            jnp.zeros_like(square),
        ]
        features[i] = jnp.concatenate(stack, axis=0).astype(BF16)[:, :MAIN]


def source_stage(raw, i, live, centre, worst, spread, moment):
    sub = lax.broadcasted_iota(jnp.int32, (8, LANES), 0)
    y = [jnp.broadcast_to(raw[c] - centre[c, pl.ds(i, 1), :], (8, LANES)) for c in range(3)]
    w = [jnp.broadcast_to(raw[3 + c], (8, LANES)) for c in range(3)]
    square = y[0] * y[0] + y[1] * y[1] + y[2] * y[2]
    reach = jnp.sqrt(square)
    size = jnp.broadcast_to(centre[3, pl.ds(i, 1), :], (8, LANES))
    ratio = (reach + size) - MOST_RATIO * jnp.maximum(reach - size, LEAST_GAP)
    worst[...] = jnp.maximum(worst[...], ratio)
    high, middle, low = split(by_quad(sub, -2.0 * y[0], -2.0 * y[1], -2.0 * y[2], square))
    one = jnp.ones_like(square)
    stack = [
        jnp.where(sub == 7, middle, high),
        jnp.where(sub < 3, high, jnp.where(sub == 3, low, jnp.where(sub == 7, one, middle))),
        jnp.where(sub % 4 == 3, one, jnp.where(sub < 4, middle, low)),
        jnp.zeros_like(square),
    ]
    spread[...] = jnp.concatenate(stack, axis=0).astype(BF16)[:, :ROWS]
    w = [live * value for value in w]
    along = y[0] * w[0] + y[1] * w[1] + y[2] * w[2]
    plain = by_quad(sub, w[0], w[1], w[2], one)
    last = [w[c] * square + along * y[c] for c in range(3)]
    front = plain * jnp.where(sub < 4, one, y[0])
    front = jnp.where(sub == 3, along, jnp.where(sub == 7, last[0], front))
    back = plain * jnp.where(sub < 4, y[1], y[2])
    back = jnp.where(sub == 3, last[1], jnp.where(sub == 7, last[2], back))
    fronts, backs = split(front), split(back)
    stack = [value for pair in zip(fronts, backs) for value in pair]
    moment[...] = jnp.concatenate(stack, axis=0).astype(BF16)[:, :ROWS]


def last_nodes(nodes, i, bodies, slots):
    y = [slots[i * COMPS + c, 0:8] for c in range(3)]
    w = [slots[i * COMPS + 3 + c, 0:8] for c in range(3)]
    sums = [[], [], []]
    for node in range(MAIN, nodes):
        d = [bodies[c][i : i + 1, node : node + 1] - y[c] for c in range(3)]
        inverse = lax.rsqrt(d[0] * d[0] + d[1] * d[1] + d[2] * d[2])
        pull = (d[0] * w[0] + d[1] * w[1] + d[2] * w[2]) * (inverse * inverse * inverse)
        for c in range(3):
            summed = jnp.sum(w[c] * inverse + d[c] * pull, axis=0, keepdims=True)
            sums[c].append(jnp.sum(summed, axis=1, keepdims=True))
    return [jnp.concatenate(values, axis=1) for values in sums]


def kernel_chunk(features, spread, kernel, low, high):
    squared = lax.dot_general(
        spread[:, low:high], features, (((0,), (0,)), ((), ())), preferred_element_type=F32
    )
    inverse = lax.rsqrt(squared)
    kernel[low:high] = (inverse * inverse * inverse).astype(BF16)


def moment_chunk(kernel, moment, low, high):
    return jnp.dot(moment[:, low:high], kernel[low:high], preferred_element_type=F32)


def near_pairs(count, target_of, source, features, total, first, second):
    def turn(q, _):
        for e, (mine, other) in enumerate(((first, second), (second, first))):
            m = 2 * q + e
            for low, high in zip(CUTS[:-1], CUTS[1:]):
                kernel_chunk(features[target_of(m)], mine[2], mine[0], low, high)
                total[target_of(m - 1)] += moment_chunk(other[0], other[1], low, high)
            source(m + 1, other[2], other[1])
        return 0

    halves = (count + 1) // 2
    second[1][...] = jnp.zeros_like(second[1])
    source(0, first[2], first[1])
    lax.fori_loop(0, halves, turn, 0)
    total[target_of(2 * halves - 1)] += moment_chunk(second[0], second[1], 0, ROWS)


def exchange_kernel(
    nodes,
    positions_in,
    weights_in,
    density_in,
    near_in,
    couplings_in,
    basis_in,
    row_geometry,
    halo_geometry,
    coupled,
    total,
    worst,
    tails,
    done_out,
    centre,
    features,
    own_geometry,
    partner_geometry,
    slots,
    positions,
    weights,
    density,
    near,
    near_scalar,
    held,
    basis,
    coef_mine,
    coef_parts,
    lists,
    mask,
    folded,
    far_mine,
    far_parts,
    chosen,
    done,
    spread0,
    spread1,
    moment0,
    moment1,
    kernel0,
    kernel1,
    load_sem,
    store_sem,
    list_send,
    list_recv,
    coef_send,
    coef_recv,
    far_send,
    far_recv,
    row_send,
    row_recv,
    halo_send,
    halo_recv,
):
    t = lax.axis_index("tgt")
    s = lax.axis_index("src")
    t_count = lax.axis_size("tgt")
    quarter = t // 4
    own = positions.shape[1]
    slot_count = near.shape[1]
    loops_back = quarter == s
    partner = s + 1 - 2 * (s % 2)

    loads = [
        pltpu.make_async_copy(source, target, load_sem.at[index])
        for index, (source, target) in enumerate(
            (
                (positions_in, positions),
                (weights_in, weights),
                (density_in, density),
                (near_in, near),
                (near_in, near_scalar),
                (basis_in, basis),
                (couplings_in, held),
            )
        )
    ]
    for load in loads:
        load.start()

    barrier = pltpu.get_barrier_semaphore()

    def greet(device):
        pl.semaphore_signal(barrier, inc=1, device_id=device, device_id_type=MESH)

    for step in range(1, 8):
        greet((t, (s + step) % 8))

    def every(act, mine):
        for k in range(t_count - 1):
            act(k + jnp.where(jnp.logical_and(loops_back, mine <= k), 1, 0))

        @pl.when(jnp.logical_not(loops_back))
        def _():
            act(t_count - 1)

    as_source = (t % 4) * 8 + s

    @pl.when(t > 0)
    def _():
        greet((t - 1, s))

    @pl.when(t < t_count - 1)
    def _():
        greet((t + 1, s))

    every(lambda k: greet((4 * s + k // 8, k % 8)), as_source)

    def block(column):
        return row_geometry.at[pl.ds(column * BLOCK, BLOCK)]

    for load in loads[:4]:
        load.wait()
    pad = jnp.zeros((own, LANES - nodes), F32)
    tails_mine = jnp.zeros((own, 128), F32)
    for c in range(COMPS):
        value = positions[c] if c < 3 else density[c - 3] * weights[...]
        value = jnp.concatenate([value, pad], axis=1)
        for k in range(TILES):
            own_geometry[c * TILES + k] = value[:, 128 * k : 128 * k + 128]
        tails_mine = tails_mine + turn_lanes(value[:, MAIN:], (nodes - MAIN) * c)
    own_geometry[COMPS * TILES] = tails_mine
    lists[s] = jnp.concatenate([near[...], jnp.full((own, 120), -1, jnp.int32)], axis=1)

    loads[5].wait()
    sub16 = lax.broadcasted_iota(jnp.int32, (16, 128), 0)
    lane16 = lax.broadcasted_iota(jnp.int32, (16, 128), 1)
    spread = jnp.zeros((16, 128), F32)
    for j in range(own):
        product = basis[j, 0].astype(F32) * density[0, j : j + 1, :]
        for c in range(1, 3):
            product = product + basis[j, c].astype(F32) * density[c, j : j + 1, :]
        value = jnp.sum(product, axis=1, keepdims=True)
        spread = jnp.where(lane16 == sub16 + 16 * j, value, spread)
    coef_mine[...] = jnp.sum(spread, axis=0, keepdims=True).astype(BF16).astype(F32)

    loads[4].wait()

    def choose(i, _):
        bodies = [near_scalar[i, k] - t * 32 for k in range(slot_count)]
        free = [jnp.where(body >= 0, 1, 0) * jnp.where(body < 32, 1, 0) for body in bodies]
        taken = [jnp.int32(0)] * slot_count
        first = 0
        for phase, count in enumerate(PHASES):
            device = (s, partner, partner, None)[phase]
            other = s * 4 + (i + 1) % own if phase in (0, 3) else partner * 4
            for e in range(count):
                pick = jnp.int32(0) + other
                live = jnp.int32(0)
                for k in range(slot_count):
                    hit = free[k] * (1 - live)
                    if device is not None:
                        hit = hit * jnp.where(bodies[k] // 4 == device, 1, 0)
                    pick = jnp.where(hit == 1, bodies[k], pick)
                    live = live + hit
                    free[k] = free[k] - hit
                    taken[k] = taken[k] + hit
                place = first * own + i * count + e
                chosen[2 * place] = pick
                chosen[2 * place + 1] = live
            first = first + count
        for k in range(slot_count):
            done[i, k] = taken[k]
        return 0

    lax.fori_loop(0, own, choose, 0)
    keep_done = pltpu.make_async_copy(done, done_out, store_sem)
    keep_done.start()

    bodies = body_rows(nodes, lambda k: own_geometry[k])
    target_stage(nodes, own, bodies, centre, features)
    total[...] = jnp.zeros_like(total)
    worst[...] = jnp.full_like(worst, -1.0)
    for k in range(own * COMPS):
        slots[k] = jnp.full((8, LANES), FAR_AWAY if k % COMPS < 3 else 0.0, F32)
    kernel1[...] = jnp.zeros_like(kernel1)

    pl.semaphore_wait(
        barrier,
        7
        + t_count
        - jnp.where(loops_back, 1, 0)
        + jnp.where(t > 0, 1, 0)
        + jnp.where(t < t_count - 1, 1, 0),
    )

    def partner_copy():
        return remote(
            own_geometry, partner_geometry, row_send.at[0], row_recv.at[0], (t, partner)
        )

    def row_copy(turn, step, source, column, device):
        return remote(
            source,
            block(column),
            row_send.at[turn * 3 + step],
            row_recv.at[turn * 3 + step],
            (t, device),
        )

    def halo_copy(side, index, source, column):
        return remote(
            source,
            halo_geometry.at[pl.ds((side * 8 + column) * BLOCK, BLOCK)],
            halo_send.at[side * 8 + index],
            halo_recv.at[side * 8 + index],
            (t + 1 - 2 * side, s),
        )

    def halo_start(index, source, column):
        @pl.when(t < t_count - 1)
        def _():
            halo_copy(0, index, source, column).start()

        @pl.when(t > 0)
        def _():
            halo_copy(1, index, source, column).start()

    def across_start(turn, source, column):
        for step in range(1, 4):
            row_copy(turn, step, source, column, (s + 2 * step) % 8).start()
        halo_start(4 * turn, source, column)

    def across_wait(turn, source, column):
        for step in range(1, 4):
            here = (column + 8 - 2 * step) % 8
            row_copy(turn, step, source, here, partner).wait_recv()
            halo_start(4 * turn + step, block(here), here)

    def coef_copy(k):
        return remote(
            coef_mine,
            coef_parts.at[(t % 4) * 8 + s],
            coef_send.at[k],
            coef_recv.at[(t % 4) * 8 + s],
            (k, quarter),
        )

    def list_copy(step):
        return remote(
            lists.at[s],
            lists.at[s],
            list_send.at[step - 1],
            list_recv.at[step - 1],
            (t, (s + step) % 8),
        )

    partner_copy().start()
    every(lambda k: coef_copy(k).start(), t)
    across_start(0, own_geometry, s)
    for step in range(1, 8):
        list_copy(step).start()

    @pl.when(loops_back)
    def _():
        coef_parts[(t % 4) * 8 + s] = coef_mine[...]

    first_set = (kernel0, moment0, spread0)
    second_set = (kernel1, moment1, spread1)

    def early_pairs(phase, geometry, device):
        count = PHASES[phase]
        first = sum(PHASES[:phase])
        last = own * count - 1

        def source(m, spread, moment):
            now = jnp.minimum(m, last)
            i = now // count
            e = now % count
            place = first * own + now
            body = chosen[2 * place]
            live = chosen[2 * place + 1].astype(F32)
            base = 0 if device is not None else (body // 4) * BLOCK
            raw = body_rows(nodes, lambda k: geometry[base + k, pl.ds(body % 4, 1), :])
            for c in range(3):
                slots[i * COMPS + c, pl.ds(first + e, 1), :] = raw[c]
                slots[i * COMPS + 3 + c, pl.ds(first + e, 1), :] = raw[3 + c] * live
            scale = live * jnp.where(m <= last, F32(1.0), F32(0.0))
            source_stage(raw, i, scale, centre, worst, spread, moment)

        def target_of(m):
            return jnp.clip(m, 0, last) // count

        near_pairs(last + 1, target_of, source, features, total, first_set, second_set)

    early_pairs(0, own_geometry, s)

    across_wait(0, own_geometry, s)
    partner_copy().wait_recv()
    across_start(1, partner_geometry, partner)
    for k in range(BLOCK):
        row_geometry[s * BLOCK + k] = own_geometry[k]
        row_geometry[partner * BLOCK + k] = partner_geometry[k]

    early_pairs(1, partner_geometry, partner)

    for step in range(1, 8):
        remote(
            lists.at[s],
            lists.at[(s + 8 - step) % 8],
            list_send.at[step - 1],
            list_recv.at[step - 1],
            (t, partner),
        ).wait_recv()
    rows = 8 * own
    listed = lists[...].reshape(rows, 128)
    ids = s * 128 + lax.broadcasted_iota(jnp.int32, (rows, 128), 1)
    hit = ids == t * rows + lax.broadcasted_iota(jnp.int32, (rows, 128), 0)
    for k in range(slot_count):
        hit = jnp.logical_or(hit, ids == listed[:, k : k + 1])
    mask[...] = jnp.where(hit, F32(0.0), F32(1.0))

    def coef_arrival(k):
        return remote(
            coef_mine, coef_parts.at[k], coef_send.at[k], coef_recv.at[k], (t, partner)
        )

    every(lambda k: coef_arrival(k).wait_recv(), as_source)
    gathered = coef_parts[...].reshape(t_count, 128).astype(BF16)
    from_row = lax.broadcasted_iota(jnp.int32, (t_count, 128), 0)
    to_lane = lax.broadcasted_iota(jnp.int32, (t_count, 128), 1)
    coef = jnp.zeros((16, 128), F32)
    for j in range(own):
        chooser = jnp.where(to_lane == own * from_row + j, F32(1.0), F32(0.0)).astype(BF16)
        coef = coef + lax.dot_general(
            gathered[:, 16 * j : 16 * j + 16],
            chooser,
            (((0,), (0,)), ((), ())),
            preferred_element_type=F32,
        )
    loads[6].wait()

    def fold(i, _):
        kept = coef * mask[pl.ds(i, 1), :]
        product = held[i].astype(F32) * kept[None]
        folded[pl.ds(pl.multiple_of(i * 16, 16), 16), :] = jnp.sum(product, axis=1)
        return 0

    lax.fori_loop(0, rows, fold, 0)
    for q in range(4):
        turned = folded[q * 128 : (q + 1) * 128, :].T
        far_mine[q] = jnp.sum(turned, axis=0, keepdims=True)

    def far_copy(step):
        other = (s + step) % 8
        return remote(
            far_mine.at[other // 2],
            far_parts.at[step - 1],
            far_send.at[step - 1],
            far_recv.at[step - 1],
            (t, other),
        )

    for step in range(1, 8):
        far_copy(step).start()

    across_wait(1, partner_geometry, partner)
    partner_copy().wait_send()
    for step in range(1, 4):
        row_copy(0, step, own_geometry, s, partner).wait_send()
    for step in range(1, 8):
        list_copy(step).wait_send()
    every(lambda k: coef_copy(k).wait_send(), t)
    early_pairs(2, partner_geometry, partner)

    early_pairs(3, row_geometry, None)
    for i in range(own):
        sums = last_nodes(nodes, i, bodies, slots)
        for c in range(3):
            empty = jnp.zeros((1, 128 + MAIN - nodes), F32)
            tails[c, i : i + 1, :] = jnp.concatenate([sums[c], empty], axis=1)

    for step in range(1, 8):
        far_copy(step).wait_recv()
    w = far_mine[s // 2]
    for step in range(1, 8):
        w = w + far_parts[step - 1]
    w = jnp.broadcast_to(w, (8, 128))
    coupled[...] = jnp.where(s % 2 == 1, pltpu.roll(w, 64, 1), w)


    for side in range(2):
        there = t > 0 if side == 0 else t < t_count - 1
        mine = t < t_count - 1 if side == 0 else t > 0
        columns = [
            ((s if index < 4 else partner) + 8 - 2 * (index % 4)) % 8 for index in range(8)
        ]

        @pl.when(there)
        def _():
            for index, column in enumerate(columns):
                halo_copy(side, index, own_geometry, column).wait_recv()

        @pl.when(mine)
        def _():
            for index, column in enumerate(columns):
                halo_copy(side, index, own_geometry, column).wait_send()

    for step in range(1, 4):
        row_copy(1, step, partner_geometry, partner, partner).wait_send()
    for step in range(1, 8):
        far_copy(step).wait_send()

    keep_done.wait()


def velocity_kernel(
    nodes,
    near_in,
    row_geometry,
    halo_geometry,
    coupled,
    early,
    early_worst,
    early_tail,
    done_in,
    centre,
    features,
    basis_in,
    out,
    near,
    done,
    basis,
    used,
    places,
    spread0,
    spread1,
    moment0,
    moment1,
    kernel0,
    kernel1,
    total,
    slots,
    worst,
    columns,
    load_sem,
):
    loads = [
        pltpu.make_async_copy(source, target, load_sem.at[index])
        for index, (source, target) in enumerate(
            (
                (near_in, near),
                (done_in, done),
                (basis_in, basis),
            )
        )
    ]
    for load in loads:
        load.start()
    t = lax.axis_index("tgt")
    s = lax.axis_index("src")
    own = out.shape[1]
    per_body = near.shape[1]
    total[...] = jnp.zeros_like(total)
    kernel1[...] = jnp.zeros_like(kernel1)
    bodies = body_rows(nodes, lambda k: row_geometry[s * BLOCK + k])

    for load in loads[:2]:
        load.wait()

    n = jnp.int32(0)
    for i in range(own):
        taken = jnp.int32(0)
        for slot in range(per_body):
            left = jnp.logical_and(near[i, slot] >= 0, done[i, slot] == 0)
            used[n] = i * per_body + slot
            places[n] = taken
            more = jnp.where(left, 1, 0)
            n = n + more
            taken = taken + more
    for k in range(2):
        used[n + k] = 0
        places[n + k] = 8

    worst[...] = early_worst[...]
    for k in range(own * COMPS):
        slots[k, 0:8] = jnp.full((8, LANES), FAR_AWAY if k % COMPS < 3 else 0.0, F32)

    def rows_of(body):
        inside = jnp.logical_and(body >= 0, body < 32)
        here = jnp.where(inside, body, 0)
        there = jnp.where(inside, 0, jnp.where(body < 0, body + 32, body))
        base = (here // 4) * BLOCK
        halo = (there // 4) * BLOCK
        place = body % 4
        return body_rows(
            nodes,
            lambda k: jnp.where(
                inside,
                row_geometry[base + k, pl.ds(place, 1), :],
                halo_geometry[halo + k, pl.ds(place, 1), :],
            ),
        )

    def source(m, spread, moment):
        k = used[m]
        i = k // per_body
        raw = rows_of(near[i, k % per_body] - t * 32)
        live = jnp.where(m < n, F32(1.0), F32(0.0))
        for c in range(3):
            slots[i * COMPS + c, pl.ds(places[m], 1), :] = raw[c]
            slots[i * COMPS + 3 + c, pl.ds(places[m], 1), :] = raw[3 + c] * live
        source_stage(raw, i, live, centre, worst, spread, moment)

    near_pairs(
        n,
        lambda m: used[jnp.maximum(m, 0)] // per_body,
        source,
        features,
        total,
        (kernel0, moment0, spread0),
        (kernel1, moment1, spread1),
    )

    loads[2].wait()
    row8 = lax.broadcasted_iota(jnp.int32, (8, 128), 0)
    lane8 = lax.broadcasted_iota(jnp.int32, (8, 128), 1)
    diagonal = jnp.where(lane8 // 16 == row8, coupled[...], 0.0).astype(BF16)[:, :64]
    far = []
    for c in range(3):
        flat = jnp.concatenate([basis[i, c] for i in range(own)], axis=0)
        far.append(jnp.dot(diagonal, flat, preferred_element_type=F32))

    for i in range(own):
        sums = last_nodes(nodes, i, bodies, slots)
        for c in range(3):
            tail = sums[c] + early_tail[c, i : i + 1, 0 : nodes - MAIN]
            out[c, i : i + 1, MAIN:nodes] = tail + far[c][i : i + 1, MAIN:nodes]

    crowded = jnp.max(worst[...]) > 0.0

    @pl.when(jnp.logical_not(crowded))
    def _():
        for i in range(own):
            at = total[i] + early[i]
            g = at[0:16] + at[16:32] + at[32:48]
            x = [
                bodies[c][i : i + 1, :MAIN] - centre[c, i : i + 1, :MAIN] for c in range(3)
            ]
            plain = [g[k : k + 1] for k in range(3)]
            first = [[g[b + k : b + k + 1] for k in range(3)] for b in (4, 8, 12)]
            last = [g[k : k + 1] for k in (7, 11, 15)]
            square = x[0] * x[0] + x[1] * x[1] + x[2] * x[2]
            inner = x[0] * plain[0] + x[1] * plain[1] + x[2] * plain[2] - g[3:4]
            for c in range(3):
                u = square * plain[c] + last[c] + x[c] * inner
                for k in range(3):
                    u = u - x[k] * (2.0 * first[k][c] + first[c][k])
                out[c, i : i + 1, :MAIN] = u + far[c][i : i + 1, :MAIN]

    @pl.when(crowded)
    def _():
        for i in range(own):
            for c in range(3):
                out[c, i : i + 1, :MAIN] = far[c][i : i + 1, :MAIN]

        def direct(k, _):
            i = k // per_body
            body = near[i, k % per_body]

            @pl.when(body >= 0)
            def _():
                empty = jnp.zeros((2, LANES), F32)
                rows = rows_of(body - t * 32)
                columns[...] = jnp.concatenate(rows + [empty], axis=0).T
                x = [
                    jnp.concatenate(
                        [
                            row_geometry[s * BLOCK + c * TILES + k, pl.ds(i, 1), :]
                            for k in range(TILES)
                        ],
                        axis=1,
                    )
                    for c in range(3)
                ]

                def eight(q, sums):
                    block = columns[pl.ds(pl.multiple_of(q * 8, 8), 8), :]
                    d = [x[c] - block[:, c : c + 1] for c in range(3)]
                    w = [block[:, 3 + c : 4 + c] for c in range(3)]
                    inverse = lax.rsqrt(d[0] * d[0] + d[1] * d[1] + d[2] * d[2])
                    pull = d[0] * w[0] + d[1] * w[1] + d[2] * w[2]
                    pull = pull * (inverse * inverse * inverse)
                    return tuple(sums[c] + (w[c] * inverse + d[c] * pull) for c in range(3))

                start = tuple(jnp.zeros((8, MAIN), F32) for _ in range(3))
                sums = lax.fori_loop(0, ROWS // 8, eight, start)
                for c in range(3):
                    out[c, pl.ds(i, 1), :MAIN] += jnp.sum(sums[c], axis=0, keepdims=True)

            return 0

        lax.fori_loop(0, own * per_body, direct, 0)


def local(positions, weights, density, near_source, couplings, source_basis, target_basis):
    own, _, nodes = positions.shape
    vmem = pl.BlockSpec(memory_space=pltpu.VMEM)
    hbm = pl.BlockSpec(memory_space=pltpu.HBM)
    dma = pltpu.SemaphoreType.DMA
    turned = (1, 0, 2)
    pair_buffers = [
        pltpu.VMEM((FACTORS, ROWS), BF16),
        pltpu.VMEM((FACTORS, ROWS), BF16),
        pltpu.VMEM((MOMENTS, ROWS), BF16),
        pltpu.VMEM((MOMENTS, ROWS), BF16),
        pltpu.VMEM((ROWS, MAIN), BF16),
        pltpu.VMEM((ROWS, MAIN), BF16),
    ]
    moved = pl.pallas_call(
        functools.partial(exchange_kernel, nodes),
        out_shape=(
            pltpu.VMEM((8 * BLOCK, own, 128), F32),
            pltpu.VMEM((16 * BLOCK, own, 128), F32),
            pltpu.VMEM((8, 128), F32),
            pltpu.VMEM((own, MOMENTS, MAIN), F32),
            pltpu.VMEM((8, LANES), F32),
            pltpu.VMEM((3, own, 128), F32),
            pltpu.VMEM((own, 8), jnp.int32),
            pltpu.VMEM((4, own, LANES), F32),
            pltpu.VMEM((own, FACTORS, MAIN), BF16),
        ),
        in_specs=[hbm] * 6,
        out_specs=(vmem,) * 9,
        scratch_shapes=[
            pltpu.VMEM((BLOCK, own, 128), F32),
            pltpu.VMEM((BLOCK, own, 128), F32),
            pltpu.VMEM((own * COMPS, 8, LANES), F32),
            pltpu.VMEM((3, own, nodes), F32),
            pltpu.VMEM((own, nodes), F32),
            pltpu.VMEM((3, own, nodes), F32),
            pltpu.VMEM((own, 8), jnp.int32),
            pltpu.SMEM((own, 8), jnp.int32),
            pltpu.VMEM((32, 16, 16, 128), BF16),
            pltpu.VMEM((own, 3, 16, nodes), BF16),
            pltpu.VMEM((1, 128), F32),
            pltpu.VMEM((32, 1, 128), F32),
            pltpu.VMEM((8, own, 128), jnp.int32),
            pltpu.VMEM((32, 128), F32),
            pltpu.VMEM((512, 128), F32),
            pltpu.VMEM((4, 1, 128), F32),
            pltpu.VMEM((7, 1, 128), F32),
            pltpu.SMEM((2 * own * EARLY,), jnp.int32),
            pltpu.SMEM((own, 8), jnp.int32),
            *pair_buffers,
            dma((7,)),
            dma,
            dma((7,)),
            dma((7,)),
            dma((32,)),
            dma((32,)),
            dma((7,)),
            dma((7,)),
            dma((7,)),
            dma((7,)),
            dma((16,)),
            dma((16,)),
        ],
        compiler_params=pltpu.CompilerParams(
            collective_id=0, has_side_effects=True, vmem_limit_bytes=VMEM_BYTES
        ),
        name="exchange",
    )(
        positions.transpose(turned),
        weights,
        density.transpose(turned),
        near_source,
        couplings.transpose(0, 2, 3, 1),
        source_basis.transpose(0, 2, 1, 3),
    )
    out = pl.pallas_call(
        functools.partial(velocity_kernel, nodes),
        out_shape=jax.ShapeDtypeStruct((3, own, nodes), F32),
        in_specs=[hbm] + [vmem] * 9 + [hbm],
        out_specs=vmem,
        scratch_shapes=[
            pltpu.SMEM((own, 8), jnp.int32),
            pltpu.SMEM((own, 8), jnp.int32),
            pltpu.VMEM((own, 3, 16, nodes), BF16),
            pltpu.SMEM((40,), jnp.int32),
            pltpu.SMEM((40,), jnp.int32),
            *pair_buffers,
            pltpu.VMEM((own, MOMENTS, MAIN), F32),
            pltpu.VMEM((own * COMPS, 16, LANES), F32),
            pltpu.VMEM((8, LANES), F32),
            pltpu.VMEM((LANES, 8), F32),
            dma((3,)),
        ],
        compiler_params=pltpu.CompilerParams(vmem_limit_bytes=VMEM_BYTES // 2),
        name="velocity",
    )(
        near_source,
        *moved,
        target_basis.transpose(0, 2, 1, 3),
    )
    return out.transpose(turned)


def solution(mesh):
    placed = (
        P(("tgt", "src"), None, None),
        P(("tgt", "src"), None),
        P(("tgt", "src"), None, None),
        P(("tgt", "src"), None),
        P("tgt", "src", None, None),
        P(("tgt", "src"), None, None, None),
        P(("tgt", "src"), None, None, None),
    )
    return jax.shard_map(
        local, mesh=mesh, in_specs=placed, out_specs=P(("tgt", "src"), None, None), check_vma=False
    )
```
